32 devices in a mesh: groups: 2 (over x), replica: 8 (over z, y), tensor: 2 (over core).
Axes of the slice: x: 2, y: 2, z: 4, core: 2. Of those that a mesh axis runs over, the one named last changes fastest.
Arguments:
- tokens: bfloat16 [6144, 8192], P(('groups', 'replica')), parts along dimension 0, may hold values from -6 to 6
- queries: bfloat16 [6144, 4096], P(('groups', 'replica'), 'tensor'), parts along dimension 0, may hold values from -56 to 56
- stored_key_cache: bfloat16 [64, 2048, 512], P(('groups', 'replica'), None, 'tensor'), parts along dimension 0, may hold values from -6 to 6
- stored_value_cache: bfloat16 [64, 2048, 512], P(('groups', 'replica'), None, 'tensor'), parts along dimension 0, may hold values from -6 to 6
- key_weight_matrix: bfloat16 [8192, 512], P(None, 'tensor'), may hold values from -0.0625 to 0.0625
- value_weight_matrix: bfloat16 [8192, 512], P(None, 'tensor'), may hold values from -0.0625 to 0.0625
- adapter_down_weight: bfloat16 [16, 8192, 128], P('replica', 'tensor'), may hold values from -0.0625 to 0.0625
- adapter_up_weight: bfloat16 [16, 2, 64, 512], P('replica', None, None, 'tensor'), may hold values from -0.75 to 0.75
- adapter_slot_index: int32 [32], P('groups'), parts along dimension 0, may hold values from 0 to 15, as said below
- request_adapter_index: int32 [16, 4], P('groups'), parts along dimension 0, may hold values from 0 to 15, as said below
- fresh_token_count: int32 [16, 4], P(('groups', 'replica')), parts along dimension 0, may hold values from 1 to 128, 384 in all within a row
- cache_token_length: int32 [16, 4], P(('groups', 'replica')), parts along dimension 0, may hold values from 256 to 2048, as said below
Outputs:
- context: bfloat16 [6144, 4096], P(('groups', 'replica'), 'tensor'), parts along dimension 0
- new_keys: bfloat16 [6144, 512], P(('groups', 'replica'), 'tensor'), parts along dimension 0
- new_values: bfloat16 [6144, 512], P(('groups', 'replica'), 'tensor'), parts along dimension 0
The draws below stay inside these ranges and needn't reach their ends.
There are 2 independent parts, one for each index of `groups`. The reference program is written for one: setup_inputs(seed, part) draws one part's arguments, and reference() takes and returns one part's arrays. A program takes and returns all parts, laid end to end along the dimension named above; an argument that names none is the same for every part. Nothing has to cross between parts.
Inputs may be any that keep to these rules, and one draw needn't show every extreme that they name: `adapter_slot_index`: a permutation: each slot holds one adapter. `request_adapter_index`: the 4 requests of one replica use adapters whose slots lie on 4 different replicas (slot // 2). `fresh_token_count`: the counts of one replica sum to 384. `cache_token_length`: some request holds exactly 2048 cached tokens.
All inputs are finite; a program needn't handle non-finite values.
Results may differ from the reference program's by a relative error of at most 0.0089.
Values may be sent and summed in bfloat16 or wider, within the bound.
No kernel may reach another device: no remote copies, remote signals or barrier semaphores. Data moves between devices by JAX's collectives and lax.ppermute only.
A program may use at most 320 MiB of HBM per device.

```python
import math
import jax
import jax.numpy as jnp
import numpy as np
from jax import lax

MODEL_WIDTH = 8192
HEAD_SIZE = 128
QH = 32
KEY_HEADS = 4
ADAPTER_RANK = 64
REQ_DEV = 4
ADPT_DEV = 2
TOK_DEV = 384
CACHE = 2048
MOST_TOK = 128
TOKENS = 3072
ADAPTER_COUNT = 16
N_REPLICA = 8


def slot_order(key):
    return jax.random.permutation(key, ADAPTER_COUNT).astype(jnp.int32)


def draw_adapter_slot_index(key, part):
    return slot_order(key)


def draw_request_adapter_index(key, part):
    table = slot_order(key)
    key = jax.random.fold_in(key, 2)
    key_hot, key_noise, key_place = jax.random.split(key, 3)
    popular_order = jax.random.permutation(key_hot, N_REPLICA)
    extra_score = jnp.where(popular_order < 2, 1 << 18, 0).astype(jnp.int32)
    random_jitter = jax.random.randint(key_noise, (N_REPLICA, N_REPLICA), 0, 1 << 18).astype(jnp.int32)
    attention_scores = (random_jitter + extra_score[None, :]) * N_REPLICA + jnp.arange(N_REPLICA, dtype=jnp.int32)[None, :]
    unused, owners = lax.top_k(attention_scores, REQ_DEV)
    places = jax.random.randint(key_place, (N_REPLICA, REQ_DEV), 0, ADPT_DEV).astype(jnp.int32)
    slots = owners.astype(jnp.int32) * ADPT_DEV + places
    inverse = jnp.argsort(table).astype(jnp.int32)
    return inverse[slots].astype(jnp.int32)


def draw_cache_token_length(key, part):
    key = jax.random.fold_in(key, 3)
    key_len, key_pick = jax.random.split(key)
    lengths = jax.random.randint(key_len, (N_REPLICA * REQ_DEV,), CACHE // 8, CACHE + 1).astype(jnp.int32)
    picked_slots = jax.random.randint(key_pick, (), 0, N_REPLICA * REQ_DEV)
    lengths = jnp.where(jnp.arange(N_REPLICA * REQ_DEV) == picked_slots, CACHE, lengths)
    return lengths.reshape(N_REPLICA, REQ_DEV).astype(jnp.int32)


def draw_queries(key, part):
    key = jax.random.fold_in(key, 4)
    key_base = jax.random.fold_in(key, 0)
    return jnp.clip(jax.random.normal(key_base, (TOKENS, QH * HEAD_SIZE), jnp.float32), -4.0, 4.0).astype(jnp.bfloat16)


def block_scale(stream_key, shape, cuts, least, high):
    loudness, own = 1.0, jax.random.fold_in(stream_key, 6)
    for axis_at, blocks in cuts:
        heights = jnp.exp(jax.random.uniform(jax.random.fold_in(own, axis_at), (blocks,), jnp.float32, least / len(cuts), high / len(cuts)))
        loudness = loudness * jnp.repeat(heights, shape[axis_at] // blocks).reshape([-1 if axis == axis_at else 1 for axis in range(len(shape))])
    return loudness


def split_up(number_of, total, bound, slope):
    portions = [(1 << 20) // math.isqrt(standing ** slope) + 1 for standing in range(2, number_of + 1)]
    rest, given = total - bound - (number_of - 1), [1] * (number_of - 1)
    while rest > 0:
        free = [i for i in range(number_of - 1) if given[i] < bound]
        pool, remaining = sum([portions[i] for i in free]), rest
        for i in free:
            addition = min(bound - given[i], max(1, remaining * portions[i] // pool), rest)
            given[i] = given[i] + addition
            rest = rest - addition
    return np.array([bound] + given)


def ragged_sizes(stream_key, amount, total, limit, skew):
    if amount == 2:
        one = jax.random.randint(stream_key, (), max(1, total - limit), min(limit, total - 1) + 1)
        return jnp.stack([one, total - one])
    sizes = jnp.asarray(split_up(amount, total, limit, skew), jnp.int32)
    twos = (amount - 1) // 2
    donor, receiver = sizes[1:1 + 2 * twos:2], sizes[2:2 + 2 * twos:2]
    slack = jnp.minimum(donor - 1, limit - receiver)
    passed = jax.random.randint(jax.random.fold_in(stream_key, 1), (twos,), 0, 1 << 20) % (slack + 1)
    sizes = sizes.at[1:1 + 2 * twos:2].set(donor - passed).at[2:2 + 2 * twos:2].set(receiver + passed)
    return sizes[jax.random.permutation(jax.random.fold_in(stream_key, 2), amount)]


def bell_draw(stream_key, dims, deviation, most, shards=(), kind=jnp.bfloat16):
    result = jax.random.normal(stream_key, dims, jnp.float32) * deviation
    if len(shards) > 0:
        result = block_scale(stream_key, dims, shards, -0.22, 0.18) * result
    return jnp.clip(result, min=-most, max=most).astype(kind)


def setup_inputs(seed: int = 0, part: int = 0) -> dict:
    arg_keys = jax.random.split(jax.random.key(seed), 13)
    part_splits = jax.random.split(jax.random.fold_in(arg_keys[12], part), 13)
    return {
        "tokens": bell_draw(part_splits[0], (TOKENS, MODEL_WIDTH), 1.0, 6.0, ((0, 8),)),
        "queries": draw_queries(jax.random.fold_in(jax.random.fold_in(arg_keys[12], part), 71), part),
        "stored_key_cache": bell_draw(part_splits[2], (N_REPLICA * REQ_DEV, CACHE, KEY_HEADS * HEAD_SIZE), 1.0, 6.0, ((0, 8), (2, 2))),
        "stored_value_cache": bell_draw(part_splits[3], (N_REPLICA * REQ_DEV, CACHE, KEY_HEADS * HEAD_SIZE), 1.0, 6.0, ((0, 8), (2, 2))),
        "key_weight_matrix": bell_draw(arg_keys[4], (MODEL_WIDTH, KEY_HEADS * HEAD_SIZE), MODEL_WIDTH ** -0.5, 0.0625, ((1, 2),)),
        "value_weight_matrix": bell_draw(arg_keys[5], (MODEL_WIDTH, KEY_HEADS * HEAD_SIZE), MODEL_WIDTH ** -0.5, 0.0625, ((1, 2),)),
        "adapter_down_weight": bell_draw(arg_keys[6], (ADAPTER_COUNT, MODEL_WIDTH, 2 * ADAPTER_RANK), MODEL_WIDTH ** -0.5, 0.0625, ((0, 8), (1, 2))),
        "adapter_up_weight": bell_draw(arg_keys[7], (ADAPTER_COUNT, 2, ADAPTER_RANK, KEY_HEADS * HEAD_SIZE), ADAPTER_RANK ** -0.5, 0.75, ((0, 8), (3, 2))),
        "adapter_slot_index": draw_adapter_slot_index(jax.random.fold_in(jax.random.fold_in(arg_keys[12], part), 71), part),
        "request_adapter_index": draw_request_adapter_index(jax.random.fold_in(jax.random.fold_in(arg_keys[12], part), 71), part),
        "fresh_token_count": jax.vmap(lambda own: ragged_sizes(own, REQ_DEV, TOK_DEV, MOST_TOK, 2))(jax.random.split(part_splits[10], N_REPLICA)).reshape((N_REPLICA, REQ_DEV)).astype(jnp.int32),
        "cache_token_length": draw_cache_token_length(jax.random.fold_in(jax.random.fold_in(arg_keys[12], part), 71), part),
    }


ADAPTER_SCALE = 0.5
THETA = 500000.0


def rotate(vectors, positions):
    half_dim = HEAD_SIZE // 2
    frequency = THETA ** (-(jnp.arange(half_dim, dtype=jnp.float32) * 2.0) / HEAD_SIZE)
    angles = positions.astype(jnp.float32)[..., None] * frequency
    cosine = jnp.cos(angles)[..., None, :]
    sine_part = jnp.sin(angles)[..., None, :]
    front_part = vectors[..., :half_dim]
    back_part = vectors[..., half_dim:]
    return jnp.concatenate([front_part * cosine - back_part * sine_part, back_part * cosine + front_part * sine_part], axis=-1)


def attend(query_rows, fresh_keys, fresh_values, cache_key, cache_value, cache_length, live_count):
    most_rows = query_rows.shape[0]
    score_scale = HEAD_SIZE ** -0.5
    query_wide = query_rows.astype(jnp.float32)
    cached = jnp.einsum("mkgd,ckd->mkgc", query_wide, cache_key.astype(jnp.float32)) * score_scale
    cached = jnp.where(jnp.arange(cache_key.shape[0]) < cache_length, cached, -1e30)
    offsets = jnp.arange(most_rows)
    allowed = (offsets[None, :] <= offsets[:, None]) & (offsets[None, :] < live_count)
    recent = jnp.einsum("mkgd,nkd->mkgn", query_wide, fresh_keys.astype(jnp.float32)) * score_scale
    recent = jnp.where(allowed[:, None, None, :], recent, -1e30)
    row_top = jnp.maximum(jnp.max(cached, axis=-1), jnp.max(recent, axis=-1))[..., None]
    cached_exp = jnp.exp(cached - row_top)
    recent_exp = jnp.exp(recent - row_top)
    denominator = jnp.sum(cached_exp, axis=-1) + jnp.sum(recent_exp, axis=-1)
    summed = jnp.einsum("mkgc,ckd->mkgd", cached_exp.astype(jnp.bfloat16).astype(jnp.float32), cache_value.astype(jnp.float32))
    summed = summed + jnp.einsum("mkgn,nkd->mkgd", recent_exp.astype(jnp.bfloat16).astype(jnp.float32), fresh_values.astype(jnp.float32))
    return summed / denominator[..., None]


def reference(tokens, queries, stored_key_cache, stored_value_cache, key_weight_matrix, value_weight_matrix, adapter_down_weight, adapter_up_weight, adapter_slot_index, request_adapter_index, fresh_token_count, cache_token_length):
    most_rows = TOK_DEV // 3
    group_size = QH // KEY_HEADS
    slot_table = adapter_slot_index[request_adapter_index]
    offsets = jnp.arange(most_rows, dtype=jnp.int32)

    def one_replica(replica_id):
        token_block = lax.dynamic_slice_in_dim(tokens, replica_id * TOK_DEV, TOK_DEV, 0)
        query_block = lax.dynamic_slice_in_dim(queries, replica_id * TOK_DEV, TOK_DEV, 0)
        counts = fresh_token_count[replica_id]
        lengths = cache_token_length[replica_id]
        local_slot_count = slot_table[replica_id]
        starts = (jnp.cumsum(counts) - counts).astype(jnp.int32)
        context = jnp.zeros((TOK_DEV, QH * HEAD_SIZE), jnp.float32)
        keys_out = jnp.zeros((TOK_DEV, KEY_HEADS * HEAD_SIZE), jnp.float32)
        values_out = jnp.zeros((TOK_DEV, KEY_HEADS * HEAD_SIZE), jnp.float32)
        for request_number in range(REQ_DEV):
            live_mask = (offsets < counts[request_number])[:, None]
            row_index = jnp.minimum(starts[request_number] + offsets, TOK_DEV - 1).astype(jnp.int32)
            token_input_rows = token_block[row_index]
            down_matrix = adapter_down_weight[local_slot_count[request_number]]
            up_matrix = adapter_up_weight[local_slot_count[request_number]]
            reduced_rank_state = jnp.dot(token_input_rows, down_matrix, preferred_element_type=jnp.float32).astype(jnp.bfloat16)
            key_linear_output = jnp.dot(token_input_rows, key_weight_matrix, preferred_element_type=jnp.float32) + ADAPTER_SCALE * jnp.dot(reduced_rank_state[:, :ADAPTER_RANK], up_matrix[0], preferred_element_type=jnp.float32)
            value_linear_output = jnp.dot(token_input_rows, value_weight_matrix, preferred_element_type=jnp.float32) + ADAPTER_SCALE * jnp.dot(reduced_rank_state[:, ADAPTER_RANK:], up_matrix[1], preferred_element_type=jnp.float32)
            positions = (lengths[request_number] + offsets).astype(jnp.int32)
            fresh_keys = rotate(key_linear_output.reshape(most_rows, KEY_HEADS, HEAD_SIZE), positions).astype(jnp.bfloat16)
            fresh_values = value_linear_output.reshape(most_rows, KEY_HEADS, HEAD_SIZE).astype(jnp.bfloat16)
            query_rows = query_block[row_index].reshape(most_rows, KEY_HEADS, group_size, HEAD_SIZE)
            block_id = replica_id * REQ_DEV + request_number
            cache_key = stored_key_cache[block_id].reshape(CACHE, KEY_HEADS, HEAD_SIZE)
            cache_value = stored_value_cache[block_id].reshape(CACHE, KEY_HEADS, HEAD_SIZE)
            context_rows = attend(query_rows, fresh_keys, fresh_values, cache_key, cache_value, lengths[request_number], counts[request_number]).reshape(most_rows, QH * HEAD_SIZE)
            context = context.at[row_index].add(jnp.where(live_mask, context_rows, 0.0))
            keys_out = keys_out.at[row_index].add(jnp.where(live_mask, fresh_keys.reshape(most_rows, KEY_HEADS * HEAD_SIZE).astype(jnp.float32), 0.0))
            values_out = values_out.at[row_index].add(jnp.where(live_mask, fresh_values.reshape(most_rows, KEY_HEADS * HEAD_SIZE).astype(jnp.float32), 0.0))
        return context.astype(jnp.bfloat16), keys_out.astype(jnp.bfloat16), values_out.astype(jnp.bfloat16)

    context_all, keys_all, values_all = lax.map(one_replica, jnp.arange(N_REPLICA, dtype=jnp.int32))
    return (context_all.reshape(TOKENS, QH * HEAD_SIZE), keys_all.reshape(TOKENS, KEY_HEADS * HEAD_SIZE), values_all.reshape(TOKENS, KEY_HEADS * HEAD_SIZE))
```

```python
import functools

import jax
import jax.numpy as jnp
import numpy as np
from jax import lax
from jax.experimental import pallas as pl
from jax.experimental.pallas import tpu as pltpu
from jax.sharding import PartitionSpec as P

HEAD = 128
GROUP = 8
RANK = 64
REQ = 4
SCALE = 0.5
THETA = 500000.0
LOG2E = 1.4426950408889634
NEG = -1e30
TILE = 32
CHUNK = 512
VMEM = 48 * 1024 * 1024


def params(*sem):
    return pltpu.CompilerParams(
        dimension_semantics=sem if sem else None, vmem_limit_bytes=VMEM
    )


def nt_dot(a, b):
    return lax.dot_general(a, b, (((1,), (1,)), ((), ())), preferred_element_type=jnp.float32)


def cached_kernel(info, q_ref, k_ref, v_ref, acc_ref, stat_ref):
    r = pl.program_id(0)
    rows_all = q_ref.shape[0]
    start = info[0, r]
    count = info[1, r]
    length = info[3, r]
    base0 = (start // 16) * 16
    tiles = (start + count - base0 + TILE - 1) // TILE
    chunks = (length + CHUNK - 1) // CHUNK
    factor = HEAD**-0.5 * LOG2E
    key_iota = lax.broadcasted_iota(jnp.int32, (1, CHUNK), 1)
    row_iota = lax.broadcasted_iota(jnp.int32, (TILE, 128), 0)
    lane = lax.broadcasted_iota(jnp.int32, (TILE, 128), 1)

    def tile(t, carry):
        base = pl.multiple_of(jnp.minimum(base0 + t * TILE, rows_all - TILE), 16)
        qt = q_ref[pl.ds(base, TILE), :]
        q = jnp.concatenate([qt[:, h * HEAD : (h + 1) * HEAD] for h in range(GROUP)], axis=0)

        def chunk(j, state):
            m, l, acc = state
            at = pl.multiple_of(j * CHUNK, CHUNK)
            s = nt_dot(q, k_ref[0, pl.ds(at, CHUNK), :])
            s = s * factor + jnp.where(key_iota + at < length, 0.0, NEG)
            top = jnp.maximum(m, jnp.max(s, axis=1, keepdims=True))
            p = jnp.exp2(s - top[:, :1])
            alpha = jnp.exp2(m - top)
            l = l * alpha + jnp.sum(p, axis=1, keepdims=True)
            acc = acc * alpha + jnp.dot(
                p.astype(jnp.bfloat16),
                v_ref[0, pl.ds(at, CHUNK), :],
                preferred_element_type=jnp.float32,
            )
            return top, l, acc

        many = TILE * GROUP
        m, l, acc = lax.fori_loop(
            0,
            chunks,
            chunk,
            (
                jnp.full((many, HEAD), NEG, jnp.float32),
                jnp.zeros((many, HEAD), jnp.float32),
                jnp.zeros((many, HEAD), jnp.float32),
            ),
        )
        at_row = row_iota + base
        mine = (at_row >= start) & (at_row < start + count)
        rows = pl.ds(base, TILE)
        stat = stat_ref[0, rows, :]
        for h in range(GROUP):
            part = slice(h * TILE, (h + 1) * TILE)
            columns = slice(h * HEAD, (h + 1) * HEAD)
            acc_ref[0, rows, columns] = jnp.where(mine, acc[part], acc_ref[0, rows, columns])
            stat = jnp.where(mine & (lane == h), m[part], stat)
            stat = jnp.where(mine & (lane == GROUP + h), l[part], stat)
        stat_ref[0, rows, :] = stat
        return carry

    lax.fori_loop(0, tiles, tile, 0)


def cached_attention(info, queries, cache_key, cache_value, head):
    rows = queries.shape[0]
    wide = GROUP * HEAD
    slots = cache_key.shape[1]
    return pl.pallas_call(
        cached_kernel,
        grid_spec=pltpu.PrefetchScalarGridSpec(
            num_scalar_prefetch=1,
            grid=(REQ,),
            in_specs=[
                pl.BlockSpec((rows, wide), lambda r, s: (0, head)),
                pl.BlockSpec((1, slots, HEAD), lambda r, s: (r, 0, head)),
                pl.BlockSpec((1, slots, HEAD), lambda r, s: (r, 0, head)),
            ],
            out_specs=[
                pl.BlockSpec((1, rows, wide), lambda r, s: (0, 0, 0)),
                pl.BlockSpec((1, rows, 128), lambda r, s: (0, 0, 0)),
            ],
        ),
        out_shape=[
            jax.ShapeDtypeStruct((1, rows, wide), jnp.float32),
            jax.ShapeDtypeStruct((1, rows, 128), jnp.float32),
        ],
        compiler_params=params("arbitrary"),
        cost_estimate=pl.CostEstimate(
            flops=2 * 2 * rows * wide * 1536, bytes_accessed=6 * 1024 * 1024, transcendentals=rows * 8 * 1536
        ),
        name="cached_attention",
    )(info, queries, cache_key, cache_value)


def low_rank_kernel(n_pieces, first, *refs):
    ids, infos = refs[0], refs[1]
    tokens = refs[2:6]
    pieces = refs[6 : 6 + n_pieces]
    rest = refs[6 + n_pieces :]
    before = rest[:4]
    outs = rest[-4:]
    rows, width = tokens[0].shape
    row_iota = lax.broadcasted_iota(jnp.int32, (rows, 1), 0)
    for n in range(4):
        outs[n][...] = jnp.zeros_like(outs[n]) if first else before[n][...]
    for p in range(n_pieces):
        for s in range(pieces[p].shape[0]):
            slot = ids[p] * pieces[p].shape[0] + s
            for n in range(4):
                for r in range(REQ):

                    @pl.when((infos[n, 8 + r] == slot) & (ids[p] >= 0))
                    def _():
                        low = jnp.dot(
                            tokens[n][...],
                            pieces[p][s, :width, :],
                            preferred_element_type=jnp.float32,
                        )
                        start = infos[n, r]
                        mine = (row_iota >= start) & (row_iota < start + infos[n, 4 + r])
                        outs[n][...] = jnp.where(mine, low, outs[n][...])


def low_rank_step(ids, infos, tokens, pieces, before):
    rows = tokens[0].shape[0]
    rank = pieces[0].shape[2]
    first = before is None
    vmem = pl.BlockSpec(memory_space=pltpu.VMEM)
    smem = pl.BlockSpec(memory_space=pltpu.SMEM)
    args = [*tokens, *pieces] + ([] if first else list(before))
    n_in = len(args)
    return pl.pallas_call(
        functools.partial(low_rank_kernel, len(pieces), first),
        in_specs=[smem, smem] + [vmem] * n_in,
        out_specs=[vmem] * 4,
        out_shape=[jax.ShapeDtypeStruct((rows, rank), jnp.float32)] * 4,
        compiler_params=params(),
        cost_estimate=pl.CostEstimate(
            flops=2 * 4 * rows * tokens[0].shape[1] * rank * len(pieces),
            bytes_accessed=6 * 1024 * 1024,
            transcendentals=0,
        ),
        name="low_rank_step",
    )(ids, infos, *args)


def final_kernel(
    info, mine_ref, other_ref, pk_ref, pv_ref, up_ref, cos_ref, sin_ref, q_ref, acc_ref, stat_ref,
    ctx_ref, ko_ref, vo_ref,
):
    rows = q_ref.shape[0]
    low = (mine_ref[...] + other_ref[...]).astype(jnp.bfloat16)
    at_row = lax.broadcasted_iota(jnp.int32, (rows, 1), 0)
    key_lin = pk_ref[...]
    value_lin = pv_ref[...]
    for r in range(REQ):
        slot = info[2, r]
        mine = (at_row >= info[0, r]) & (at_row < info[0, r] + info[1, r])
        dk = jnp.dot(low[:, :RANK], up_ref[slot, 0], preferred_element_type=jnp.float32)
        dv = jnp.dot(low[:, RANK:], up_ref[slot, 1], preferred_element_type=jnp.float32)
        key_lin = key_lin + SCALE * jnp.where(mine, dk, 0.0)
        value_lin = value_lin + SCALE * jnp.where(mine, dv, 0.0)
    turned = key_lin * cos_ref[...] + pltpu.roll(key_lin, HEAD // 2, 1) * sin_ref[...]
    keys = turned.astype(jnp.bfloat16)
    values = value_lin.astype(jnp.bfloat16)
    ko_ref[...] = keys
    vo_ref[...] = values
    factor = HEAD**-0.5 * LOG2E
    most = rows // 3
    many = most * GROUP
    for b in range(3):
        low_key = max(b - 1, 0) * most
        high_key = (b + 1) * most
        span = high_key - low_key
        q_at = lax.broadcasted_iota(jnp.int32, (most, 1), 0) + b * most
        k_at = lax.broadcasted_iota(jnp.int32, (1, span), 1) + low_key
        q_req = jnp.zeros((most, 1), jnp.int32)
        k_req = jnp.zeros((1, span), jnp.int32)
        for r in range(1, REQ):
            q_req = q_req + (q_at >= info[0, r]).astype(jnp.int32)
            k_req = k_req + (k_at >= info[0, r]).astype(jnp.int32)
        bias = jnp.where((q_req == k_req) & (k_at <= q_at), 0.0, NEG)
        part = slice(b * most, (b + 1) * most)
        for h in range(GROUP):
            columns = slice(h * HEAD, (h + 1) * HEAD)
            s = nt_dot(q_ref[part, columns], keys[low_key:high_key])
            s = s * factor + bias
            before = stat_ref[0, part, h : h + 1]
            top = jnp.maximum(before, jnp.max(s, axis=1, keepdims=True))
            p = jnp.exp2(s - top)
            alpha = jnp.exp2(before - top)
            total = stat_ref[0, part, GROUP + h : GROUP + h + 1] * alpha + jnp.sum(
                p, axis=1, keepdims=True
            )
            out = acc_ref[0, part, columns] * alpha + jnp.dot(
                p.astype(jnp.bfloat16), values[low_key:high_key], preferred_element_type=jnp.float32
            )
            ctx_ref[part, columns] = (out / total).astype(jnp.bfloat16)


def final_step(head, info, mine, other, pk, pv, up, cosine, sine, queries, acc, stat, before):
    rows = queries.shape[0]
    wide = GROUP * HEAD
    heads = queries.shape[1] // wide
    n_slots = up.shape[0]
    rank2 = mine.shape[1]
    whole = lambda shape: pl.BlockSpec(shape, lambda i, s: (0,) * len(shape))
    return pl.pallas_call(
        final_kernel,
        grid_spec=pltpu.PrefetchScalarGridSpec(
            num_scalar_prefetch=1,
            grid=(heads,),
            in_specs=[
                whole((rows, rank2)),
                whole((rows, rank2)),
                pl.BlockSpec((rows, HEAD), lambda i, s: (0, i)),
                pl.BlockSpec((rows, HEAD), lambda i, s: (0, i)),
                pl.BlockSpec((n_slots, 2, RANK, HEAD), lambda i, s: (0, 0, 0, i)),
                whole((rows, HEAD)),
                whole((rows, HEAD)),
                pl.BlockSpec((rows, wide), lambda i, s: (0, i)),
                pl.BlockSpec((1, rows, wide), lambda i, s: (i, 0, 0)),
                pl.BlockSpec((1, rows, 128), lambda i, s: (i, 0, 0)),
            ],
            out_specs=[
                pl.BlockSpec((rows, wide), lambda i, s: (0, i)),
                pl.BlockSpec((rows, HEAD), lambda i, s: (0, i)),
                pl.BlockSpec((rows, HEAD), lambda i, s: (0, i)),
            ],
        ),
        out_shape=[
            jax.ShapeDtypeStruct(queries.shape, jnp.bfloat16),
            jax.ShapeDtypeStruct((rows, heads * HEAD), jnp.bfloat16),
            jax.ShapeDtypeStruct((rows, heads * HEAD), jnp.bfloat16),
        ],
        compiler_params=params("arbitrary"),
        name="final_step",
    )(info, mine, other, pk, pv, up, cosine, sine, queries, acc, stat)


def body(
    fast,
    tokens,
    queries,
    stored_key_cache,
    stored_value_cache,
    key_weight_matrix,
    value_weight_matrix,
    adapter_down_weight,
    adapter_up_weight,
    adapter_slot_index,
    request_adapter_index,
    fresh_token_count,
    cache_token_length,
):
    group = lax.axis_index("groups")
    replica = lax.axis_index("replica")
    core = lax.axis_index("tensor")
    rows, width = tokens.shape
    held, half, rank2 = adapter_down_weight.shape
    counts = fresh_token_count[0]
    lengths = cache_token_length[0]
    starts = jnp.cumsum(counts) - counts
    wanted = lax.dynamic_index_in_dim(request_adapter_index, replica, 0, False)
    n_slots = adapter_slot_index.shape[0]
    slots = jnp.sum(
        jnp.where(
            wanted[:, None] == jnp.arange(n_slots, dtype=jnp.int32)[None, :],
            adapter_slot_index[None, :],
            0,
        ),
        axis=1,
    )
    info = jnp.stack([starts, counts, slots, lengths]).astype(jnp.int32)

    at_row = jnp.arange(rows, dtype=jnp.int32)
    of_request = jnp.sum(at_row[:, None] >= starts[None, 1:], axis=1)
    shift = lengths - starts
    position = at_row + jnp.sum(
        jnp.where(of_request[:, None] == jnp.arange(REQ)[None, :], shift[None, :], 0), axis=1
    )
    frequency = THETA ** (-(jnp.arange(HEAD // 2, dtype=jnp.float32) * 2.0) / HEAD)
    angles = position.astype(jnp.float32)[:, None] * frequency
    cosine = jnp.cos(angles)
    sine = jnp.sin(angles)
    cosine = jnp.concatenate([cosine, cosine], axis=1)
    sine = jnp.concatenate([-sine, sine], axis=1)

    n_replica = lax.axis_size("replica")
    core_swap = [(0, 1), (1, 0)]
    up_all = lax.all_gather(adapter_up_weight, "replica", axis=0, tiled=True)
    heads = key_weight_matrix.shape[1] // HEAD

    if fast:
        y = replica % 2
        column = group * 2 + y
        quarter = half // 4
        by_x = lambda a: lax.ppermute(a, "groups", [(0, 1), (1, 0)])
        by_y = lambda a: lax.ppermute(a, "replica", [(r, r ^ 1) for r in range(n_replica)])
        by_xy = lambda a: lax.ppermute(
            a,
            ("groups", "replica"),
            [
                (g * n_replica + r, (1 - g) * n_replica + (r ^ 1))
                for g in range(2)
                for r in range(n_replica)
            ],
        )
        by_z = lambda a, d: lax.ppermute(
            a,
            "replica",
            [(r, r + 2 * d) for r in range(n_replica) if 0 <= r + 2 * d < n_replica],
        )
        down_part = lambda c: lax.dynamic_slice_in_dim(
            adapter_down_weight, c * quarter, quarter, 1
        )
        own_a = down_part(column)
        own_b = by_y(down_part(column ^ 1))
        token_part = lambda c: lax.dynamic_slice_in_dim(
            tokens, core * half + c * quarter, quarter, 1
        )
        up1a = by_z(own_a, 1)
        dn1a = by_z(own_a, -1)
        t_own = token_part(column)
        t_x = by_x(token_part(column ^ 2))
        t_y = by_y(token_part(column ^ 1))
        t_d = by_xy(token_part(column ^ 3))
        flat = info[:3].reshape(-1)
        infos = jnp.stack([flat, by_x(flat), by_y(flat), by_xy(flat)])
        layer_tokens = [t_own, t_x, t_y, t_d]
        up1b = by_z(own_b, 1)
        dn1b = by_z(own_b, -1)
        up2a = by_z(up1a, 1)
        dn2a = by_z(dn1a, -1)
        up2b = by_z(up1b, 1)
        dn2b = by_z(dn1b, -1)
        up3a = by_z(up2a, 1)
        dn3a = by_z(dn2a, -1)
        up3b = by_z(up2b, 1)
        dn3b = by_z(dn2b, -1)

        def ids(*offsets):
            mates = [(replica ^ flip) + 2 * o for o, flip in offsets]
            return jnp.stack([jnp.where(m < n_replica, m, -1) for m in mates]).astype(jnp.int32)

        low = low_rank_step(
            ids((0, 0), (0, 1), (-1, 0), (1, 0), (-1, 1), (1, 1)),
            infos,
            layer_tokens,
            [own_a, own_b, up1a, dn1a, up1b, dn1b],
            None,
        )
        low = low_rank_step(
            ids((-2, 0), (2, 0), (-2, 1), (2, 1)), infos, layer_tokens, [up2a, dn2a, up2b, dn2b], low
        )
        low = low_rank_step(
            ids((-3, 0), (3, 0), (-3, 1), (3, 1)), infos, layer_tokens, [up3a, dn3a, up3b, dn3b], low
        )
        low_sum = low[0] + by_x(low[1]) + by_y(low[2]) + by_xy(low[3])
    else:
        down_all = lax.all_gather(adapter_down_weight, "replica", axis=0, tiled=True)
        mine = lax.dynamic_slice_in_dim(tokens, core * half, half, 1)
        low_sum = jnp.zeros((rows, rank2), jnp.float32)
        for r in range(REQ):
            low_sum = low_sum + jnp.where(
                (of_request == r)[:, None],
                jnp.dot(mine, down_all[slots[r]], preferred_element_type=jnp.float32),
                0.0,
            )

    plain_key = jnp.dot(tokens, key_weight_matrix, preferred_element_type=jnp.float32)
    plain_value = jnp.dot(tokens, value_weight_matrix, preferred_element_type=jnp.float32)
    parts = [
        cached_attention(info, queries, stored_key_cache, stored_value_cache, h)
        for h in range(heads)
    ]
    acc = jnp.concatenate([p[0] for p in parts])
    stat = jnp.concatenate([p[1] for p in parts])
    low_other = lax.ppermute(low_sum, "tensor", core_swap)
    return tuple(
        final_step(
            None, info, low_sum, low_other, plain_key, plain_value, up_all, cosine, sine, queries,
            acc, stat, None,
        )
    )


def layered(mesh):
    if dict(mesh.shape) != {"groups": 2, "replica": 8, "tensor": 2}:
        return False
    return True


def solution(mesh):
    rows = P(("groups", "replica"), None)
    split = P(("groups", "replica"), "tensor")
    cache = P(("groups", "replica"), None, "tensor")
    placed = (
        rows,
        split,
        cache,
        cache,
        P(None, "tensor"),
        P(None, "tensor"),
        P("replica", "tensor", None),
        P("replica", None, None, "tensor"),
        P("groups"),
        P("groups", None),
        rows,
        rows,
    )
    return jax.shard_map(
        functools.partial(body, layered(mesh)),
        mesh=mesh,
        in_specs=placed,
        out_specs=(split, split, split),
        check_vma=False,
    )
```

```python
import functools

import jax
import jax.numpy as jnp
import numpy as np
from jax import lax
from jax.experimental import pallas as pl
from jax.experimental.pallas import tpu as pltpu
from jax.sharding import PartitionSpec as P

HEAD = 128
GROUP = 8
RANK = 64
REQ = 4
SCALE = 0.5
THETA = 500000.0
LOG2E = 1.4426950408889634
NEG = -1e30
TILE = 64
CHUNK = 1024
PART = 8
ALIGN = 16
VMEM = 60 * 1024 * 1024


def params(*sem):
    return pltpu.CompilerParams(
        dimension_semantics=sem if sem else None, vmem_limit_bytes=VMEM
    )


def nt_dot(a, b):
    return lax.dot_general(a, b, (((1,), (1,)), ((), ())), preferred_element_type=jnp.float32)


def cached_kernel(info, q_ref, k_ref, v_ref, *rest):
    acc_ref, stat_ref = rest[-2:]
    r = pl.program_id(0)
    rows_all = q_ref.shape[0]
    start = info[0, r]
    count = info[1, r]
    length = info[3, r]
    base0 = (start // ALIGN) * ALIGN
    tiles = (start + count - base0 + TILE - 1) // TILE
    chunks = (length + CHUNK - 1) // CHUNK
    factor = HEAD**-0.5 * LOG2E
    key_iota = lax.broadcasted_iota(jnp.int32, (1, CHUNK), 1)
    row_iota = lax.broadcasted_iota(jnp.int32, (TILE, 128), 0)
    lane = lax.broadcasted_iota(jnp.int32, (TILE, 128), 1)
    many = TILE * PART
    lanes = [slice(i * 128, (i + 1) * 128) for i in range(CHUNK // 128)]

    def tile(t, carry):
        base = pl.multiple_of(jnp.minimum(base0 + t * TILE, rows_all - TILE), ALIGN)
        qt = q_ref[pl.ds(base, TILE), :]
        q = jnp.concatenate([qt[:, h * HEAD : (h + 1) * HEAD] for h in range(PART)], axis=0)

        def chunk(j, state):
            m, l, acc = state
            at = pl.multiple_of(j * CHUNK, CHUNK)
            s = nt_dot(q, k_ref[0, pl.ds(at, CHUNK), :])
            s = s + jnp.where(key_iota + at < length, 0.0, NEG)
            most = s[:, lanes[0]]
            for cut in lanes[1:]:
                most = jnp.maximum(most, s[:, cut])
            top = jnp.maximum(
                m, jnp.broadcast_to(jnp.max(most, axis=1, keepdims=True), (many, 128)) * factor
            )
            alpha = jnp.exp2(m - top)
            l = l * alpha
            weights = []
            for cut in lanes:
                p = jnp.exp2(s[:, cut] * factor - top)
                l = l + p
                weights.append(p.astype(jnp.bfloat16))
            acc = acc * alpha + jnp.dot(
                jnp.concatenate(weights, axis=1),
                v_ref[0, pl.ds(at, CHUNK), :],
                preferred_element_type=jnp.float32,
            )
            return top, l, acc

        m, l, acc = lax.fori_loop(
            0,
            chunks,
            chunk,
            (
                jnp.full((many, 128), NEG, jnp.float32),
                jnp.zeros((many, 128), jnp.float32),
                jnp.zeros((many, HEAD), jnp.float32),
            ),
        )
        l = jnp.sum(l, axis=1, keepdims=True)
        at_row = row_iota + base
        mine = (at_row >= start) & (at_row < start + count)
        rows = pl.ds(base, TILE)
        tops = stat_ref[0, 0, rows, :]
        sums = stat_ref[0, 1, rows, :]
        for h in range(PART):
            part = slice(h * TILE, (h + 1) * TILE)
            columns = slice(h * HEAD, (h + 1) * HEAD)
            acc_ref[0, rows, columns] = jnp.where(mine, acc[part], acc_ref[0, rows, columns])
            here = mine & (lane == h)
            tops = jnp.where(here, m[part], tops)
            sums = jnp.where(here, l[part], sums)
        stat_ref[0, 0, rows, :] = tops
        stat_ref[0, 1, rows, :] = sums
        return carry

    lax.fori_loop(0, tiles, tile, 0)


def cached_attention(info, queries, cache_key, cache_value, part, before):
    rows = queries.shape[0]
    wide = PART * HEAD
    parts = queries.shape[1] // wide
    head = part * PART // GROUP
    slots = cache_key.shape[1]
    extra = [] if before is None else list(before)
    return pl.pallas_call(
        cached_kernel,
        grid_spec=pltpu.PrefetchScalarGridSpec(
            num_scalar_prefetch=1,
            grid=(REQ,),
            in_specs=[
                pl.BlockSpec((rows, wide), lambda r, s: (0, part)),
                pl.BlockSpec((1, slots, HEAD), lambda r, s: (r, 0, head)),
                pl.BlockSpec((1, slots, HEAD), lambda r, s: (r, 0, head)),
            ]
            + [pl.BlockSpec(memory_space=pltpu.HBM)] * len(extra),
            out_specs=[
                pl.BlockSpec((1, rows, wide), lambda r, s: (part, 0, 0)),
                pl.BlockSpec((1, 2, rows, 128), lambda r, s: (part, 0, 0, 0)),
            ],
        ),
        out_shape=[
            jax.ShapeDtypeStruct((parts, rows, wide), jnp.float32),
            jax.ShapeDtypeStruct((parts, 2, rows, 128), jnp.float32),
        ],
        input_output_aliases={4: 0, 5: 1} if extra else {},
        compiler_params=params("arbitrary"),
        cost_estimate=pl.CostEstimate(
            flops=4 * rows * wide * 4096,
            bytes_accessed=6 * 1024 * 1024,
            transcendentals=rows * PART * 2048,
        ),
        name="cached_attention",
    )(info, queries, cache_key, cache_value, *extra)


def low_rank_kernel(pick, n_pieces, place, infos, *refs):
    tokens = refs[:4]
    pieces = refs[4 : 4 + n_pieces]
    before = refs[4 + n_pieces : -7]
    outs = refs[-7:-3]
    token_scr, piece_scr, sems = refs[-3:]
    rows = tokens[0].shape[0]
    held = piece_scr.shape[1]
    copies = [pltpu.make_async_copy(tokens[n], token_scr.at[n], sems.at[n]) for n in range(4)]
    at = 0
    for p in range(n_pieces):
        if len(pieces[p].shape) == 4:
            target = piece_scr.at[pl.ds(at, pieces[p].shape[0])]
            at += pieces[p].shape[0]
        else:
            target = piece_scr.at[at]
            at += 1
        copies.append(pltpu.make_async_copy(pieces[p], target, sems.at[4 + p]))
    for copy in copies:
        copy.start()
    for n in range(4):
        outs[n][...] = jnp.zeros_like(outs[n]) if pick == "early" else before[n][...]
    for copy in copies:
        copy.wait()
    window = rows // 3 + ALIGN
    row_iota = lax.broadcasted_iota(jnp.int32, (window, 1), 0)
    z, y = place[0], place[1]
    at_end = (z == 0) | (z == 3)

    for n in range(4):

        def one(r, carry):
            start = infos[n, r]
            slot = infos[n, 8 + r]
            owner = slot // held
            layer = owner // 2
            other = jnp.where(owner % 2 != y, 1, 0)
            mates = layer // 2 == z // 2
            ends = (layer == 0) | (layer == 3)
            last = at_end & ends & jnp.logical_not(mates)
            if pick == "early":
                kind = jnp.where(at_end, 4, jnp.where(ends, 3, 2))
                kind = jnp.where(mates, jnp.where(layer == z, 0, 1), kind)
                index = jnp.minimum(kind * 2 + other, piece_scr.shape[0] - 1)
                valid = jnp.logical_not(last)
            else:
                index = other
                valid = last

            @pl.when(valid)
            def _():
                base = pl.multiple_of(
                    jnp.minimum((start // ALIGN) * ALIGN, rows - window), ALIGN
                )
                span = pl.ds(base, window)
                low = jnp.dot(
                    token_scr[n, span, :],
                    piece_scr[index, slot % held],
                    preferred_element_type=jnp.float32,
                )
                mine = (row_iota + base >= start) & (row_iota + base < start + infos[n, 4 + r])
                outs[n][span, :] = jnp.where(mine, low, outs[n][span, :])

            return carry

        lax.fori_loop(0, REQ, one, 0)


def low_rank_step(pick, place, infos, tokens, pieces, before):
    rows, width = tokens[0].shape
    held, _, rank = pieces[0].shape[-3:]
    vmem = pl.BlockSpec(memory_space=pltpu.VMEM)
    smem = pl.BlockSpec(memory_space=pltpu.SMEM)
    hbm = pl.BlockSpec(memory_space=pltpu.HBM)
    total = sum(p.shape[0] if p.ndim == 4 else 1 for p in pieces)
    return pl.pallas_call(
        functools.partial(low_rank_kernel, pick, len(pieces)),
        in_specs=[smem, smem] + [hbm] * (4 + len(pieces)) + [vmem] * len(before),
        out_specs=[vmem] * 4,
        out_shape=[jax.ShapeDtypeStruct((rows, rank), jnp.float32)] * 4,
        scratch_shapes=[
            pltpu.VMEM((4, rows, width), jnp.bfloat16),
            pltpu.VMEM((total, held, width, rank), jnp.bfloat16),
            pltpu.SemaphoreType.DMA((4 + len(pieces),)),
        ],
        compiler_params=params(),
        cost_estimate=pl.CostEstimate(
            flops=2 * 4 * rows * width * rank * 4, bytes_accessed=6 * 1024 * 1024, transcendentals=0
        ),
        name="low_rank_" + pick,
    )(place, infos, *tokens, *pieces, *before)


def final_kernel(
    info, mine_ref, other_ref, pk_ref, pv_ref, up_ref, cos_ref, sin_ref, q_ref, acc_ref, stat_ref,
    ctx_ref, ko_ref, vo_ref,
):
    rows = q_ref.shape[0]

    @pl.when(pl.program_id(0) % (GROUP // PART) == 0)
    def _():
        low = (mine_ref[...] + other_ref[...]).astype(jnp.bfloat16)
        at_row = lax.broadcasted_iota(jnp.int32, (rows, 1), 0)
        key_lin = pk_ref[...]
        value_lin = pv_ref[...]
        for r in range(REQ):
            slot = info[2, r]
            mine = (at_row >= info[0, r]) & (at_row < info[0, r] + info[1, r])
            dk = jnp.dot(low[:, :RANK], up_ref[slot, 0], preferred_element_type=jnp.float32)
            dv = jnp.dot(low[:, RANK:], up_ref[slot, 1], preferred_element_type=jnp.float32)
            key_lin = key_lin + SCALE * jnp.where(mine, dk, 0.0)
            value_lin = value_lin + SCALE * jnp.where(mine, dv, 0.0)
        turned = key_lin * cos_ref[...] + pltpu.roll(key_lin, HEAD // 2, 1) * sin_ref[...]
        ko_ref[...] = turned.astype(jnp.bfloat16)
        vo_ref[...] = value_lin.astype(jnp.bfloat16)

    factor = HEAD**-0.5 * LOG2E
    most = rows // 3
    span = 2 * most

    def block(b, carry):
        low_key = pl.multiple_of(jnp.maximum(b - 1, 0) * most, most)
        at = pl.multiple_of(b * most, most)
        q_at = lax.broadcasted_iota(jnp.int32, (most, 1), 0) + at
        k_at = lax.broadcasted_iota(jnp.int32, (1, span), 1) + low_key
        q_req = jnp.zeros((most, 1), jnp.int32)
        k_req = jnp.zeros((1, span), jnp.int32)
        for r in range(1, REQ):
            q_req = q_req + (q_at >= info[0, r]).astype(jnp.int32)
            k_req = k_req + (k_at >= info[0, r]).astype(jnp.int32)
        bias = jnp.where((q_req == k_req) & (k_at <= q_at), 0.0, NEG)
        part = pl.ds(at, most)
        lane = lax.broadcasted_iota(jnp.int32, (most, 128), 1)
        heads = [slice(h * HEAD, (h + 1) * HEAD) for h in range(PART)]
        cuts = [slice(h * most, (h + 1) * most) for h in range(PART)]
        q = jnp.concatenate([q_ref[part, h] for h in heads], axis=0)
        scores = nt_dot(q, ko_ref[pl.ds(low_key, span), :])
        fresh_top = jnp.zeros((most, 128), jnp.float32)
        fresh_sum = jnp.ones((most, 128), jnp.float32)
        weights = []
        for h in range(PART):
            s = scores[cuts[h]] * factor + bias
            top = jnp.max(s, axis=1, keepdims=True)
            p = jnp.exp2(s - top)
            fresh_top = jnp.where(lane == h, top, fresh_top)
            fresh_sum = jnp.where(lane == h, jnp.sum(p, axis=1, keepdims=True), fresh_sum)
            weights.append(p.astype(jnp.bfloat16))
        fresh = jnp.dot(
            jnp.concatenate(weights, axis=0),
            vo_ref[pl.ds(low_key, span), :],
            preferred_element_type=jnp.float32,
        )
        live = lane < PART
        before = jnp.where(live, stat_ref[0, 0, part, :], 0.0)
        before_sum = jnp.where(live, stat_ref[0, 1, part, :], 1.0)
        top = jnp.maximum(before, fresh_top)
        old = jnp.exp2(before - top)
        new = jnp.exp2(fresh_top - top)
        total = before_sum * old + fresh_sum * new
        old = old / total
        new = new / total
        for h in range(PART):
            out = (
                acc_ref[0, part, heads[h]] * old[:, h : h + 1]
                + fresh[cuts[h]] * new[:, h : h + 1]
            )
            ctx_ref[part, heads[h]] = out.astype(jnp.bfloat16)
        return carry

    lax.fori_loop(0, 3, block, 0)


def final_step(info, mine, other, pk, pv, up, cosine, sine, queries, acc, stat):
    rows = queries.shape[0]
    wide = PART * HEAD
    parts = queries.shape[1] // wide
    each = GROUP // PART
    heads = parts // each
    n_slots = up.shape[0]
    rank2 = mine.shape[1]
    whole = lambda shape: pl.BlockSpec(shape, lambda i, s: (0,) * len(shape))
    of_head = pl.BlockSpec((rows, HEAD), lambda i, s: (0, i // each))
    return pl.pallas_call(
        final_kernel,
        grid_spec=pltpu.PrefetchScalarGridSpec(
            num_scalar_prefetch=1,
            grid=(parts,),
            in_specs=[
                whole((rows, rank2)),
                whole((rows, rank2)),
                of_head,
                of_head,
                pl.BlockSpec((n_slots, 2, RANK, HEAD), lambda i, s: (0, 0, 0, i // each)),
                whole((rows, HEAD)),
                whole((rows, HEAD)),
                pl.BlockSpec((rows, wide), lambda i, s: (0, i)),
                pl.BlockSpec((1, rows, wide), lambda i, s: (i, 0, 0)),
                pl.BlockSpec((1, 2, rows, 128), lambda i, s: (i, 0, 0, 0)),
            ],
            out_specs=[pl.BlockSpec((rows, wide), lambda i, s: (0, i)), of_head, of_head],
        ),
        out_shape=[
            jax.ShapeDtypeStruct(queries.shape, jnp.bfloat16),
            jax.ShapeDtypeStruct((rows, heads * HEAD), jnp.bfloat16),
            jax.ShapeDtypeStruct((rows, heads * HEAD), jnp.bfloat16),
        ],
        compiler_params=params("arbitrary"),
        name="final_step",
    )(info, mine, other, pk, pv, up, cosine, sine, queries, acc, stat)


def after(value, *others):
    return lax.optimization_barrier((value, *others))[0]


def body(
    fast,
    tokens,
    queries,
    stored_key_cache,
    stored_value_cache,
    key_weight_matrix,
    value_weight_matrix,
    adapter_down_weight,
    adapter_up_weight,
    adapter_slot_index,
    request_adapter_index,
    fresh_token_count,
    cache_token_length,
):
    group = lax.axis_index("groups")
    replica = lax.axis_index("replica")
    core = lax.axis_index("tensor")
    rows, width = tokens.shape
    held, half, rank2 = adapter_down_weight.shape
    counts = fresh_token_count[0]
    lengths = cache_token_length[0]
    order = jnp.arange(REQ, dtype=jnp.int32)
    starts = jnp.sum(jnp.where(order[:, None] > order[None, :], counts[None, :], 0), axis=1)
    wanted = lax.dynamic_index_in_dim(request_adapter_index, replica, 0, False)
    n_slots = adapter_slot_index.shape[0]
    slots = jnp.sum(
        jnp.where(
            wanted[:, None] == jnp.arange(n_slots, dtype=jnp.int32)[None, :],
            adapter_slot_index[None, :],
            0,
        ),
        axis=1,
    )
    info = jnp.stack([starts, counts, slots, lengths]).astype(jnp.int32)

    at_row = jnp.arange(rows, dtype=jnp.int32)
    of_request = jnp.sum(at_row[:, None] >= starts[None, 1:], axis=1)
    shift = lengths - starts
    position = at_row + jnp.sum(
        jnp.where(of_request[:, None] == jnp.arange(REQ)[None, :], shift[None, :], 0), axis=1
    )
    frequency = THETA ** (-(jnp.arange(HEAD // 2, dtype=jnp.float32) * 2.0) / HEAD)
    angles = position.astype(jnp.float32)[:, None] * frequency
    cosine = jnp.cos(angles)
    sine = jnp.sin(angles)
    cosine = jnp.concatenate([cosine, cosine], axis=1)
    sine = jnp.concatenate([-sine, sine], axis=1)

    n_replica = lax.axis_size("replica")
    up_all = lax.all_gather(adapter_up_weight, "replica", axis=0, tiled=True)

    if fast:
        y = replica % 2
        column = group * 2 + y
        quarter = half // 4
        by_x = lambda a: lax.ppermute(a, "groups", [(0, 1), (1, 0)])
        by_y = lambda a: lax.ppermute(a, "replica", [(r, r ^ 1) for r in range(n_replica)])
        by_xy = lambda a: lax.ppermute(
            a,
            ("groups", "replica"),
            [
                (g * n_replica + r, (1 - g) * n_replica + (r ^ 1))
                for g in range(2)
                for r in range(n_replica)
            ],
        )
        mesh_z = lambda a, pairs: lax.ppermute(
            a, "replica", [(2 * f + p, 2 * t + p) for f, t in pairs for p in range(2)]
        )
        in_pair = lambda a: mesh_z(a, [(0, 1), (1, 0), (2, 3), (3, 2)])
        across = lambda a: mesh_z(a, [(1, 2), (2, 1)])
        outward = lambda a: mesh_z(a, [(1, 0), (2, 3)])
        down_part = lambda c: lax.dynamic_slice_in_dim(
            adapter_down_weight, c * quarter, quarter, 1
        )
        own_b = by_y(down_part(column ^ 1))
        own_a = down_part(column)
        pair_a = in_pair(own_a)
        mid_a = across(own_a)
        flat = info[:3].reshape(-1)
        infos = jnp.stack([flat, by_x(flat), by_y(flat), by_xy(flat)])
        token_part = lambda c: lax.dynamic_slice_in_dim(
            tokens, core * half + c * quarter, quarter, 1
        )
        layer_tokens = [
            token_part(column),
            by_x(token_part(column ^ 2)),
            by_y(token_part(column ^ 1)),
            by_xy(token_part(column ^ 3)),
        ]
        plain_key = jnp.dot(tokens, key_weight_matrix, preferred_element_type=jnp.float32)
        plain_value = jnp.dot(tokens, value_weight_matrix, preferred_element_type=jnp.float32)
        own_b = after(own_b, plain_key, plain_value)
        pair_b = in_pair(own_b)
        mid_b = across(own_b)
        part = lambda n, q, b: cached_attention(
            info, q, stored_key_cache, stored_value_cache, n, b
        )
        across_2 = across(jnp.stack([pair_a, pair_b]))
        outward_2 = outward(jnp.stack([mid_a, mid_b]))
        cached = part(0, after(queries, pair_b, mid_b), None)
        outward_3 = outward(after(across_2, cached[0]))
        cached = part(1, after(queries, across_2, outward_2, *layer_tokens, infos), cached)
        place = jnp.stack([replica // 2, y]).astype(jnp.int32)
        early = [own_a, own_b, pair_a, pair_b, mid_a, mid_b, across_2, outward_2]
        low = low_rank_step("early", place, infos, layer_tokens, early, [])
        low = list(low)
        outward_3 = after(outward_3, cached[0])
        low = low_rank_step("late", place, infos, layer_tokens, [outward_3], low)
        low_sum = low[0] + by_x(low[1]) + by_y(low[2]) + by_xy(low[3])
    else:
        down_all = lax.all_gather(adapter_down_weight, "replica", axis=0, tiled=True)
        mine = lax.dynamic_slice_in_dim(tokens, core * half, half, 1)
        low_sum = jnp.zeros((rows, rank2), jnp.float32)
        for r in range(REQ):
            low_sum = low_sum + jnp.where(
                (of_request == r)[:, None],
                jnp.dot(mine, down_all[slots[r]], preferred_element_type=jnp.float32),
                0.0,
            )
        plain_key = jnp.dot(tokens, key_weight_matrix, preferred_element_type=jnp.float32)
        plain_value = jnp.dot(tokens, value_weight_matrix, preferred_element_type=jnp.float32)
        cached = None
        for n in range(queries.shape[1] // (PART * HEAD)):
            cached = cached_attention(
                info, queries, stored_key_cache, stored_value_cache, n, cached
            )
    low_other = lax.ppermute(low_sum, "tensor", [(0, 1), (1, 0)])
    return tuple(
        final_step(
            info, low_sum, low_other, plain_key, plain_value, up_all, cosine, sine, queries, *cached
        )
    )


def layered(mesh):
    return dict(mesh.shape) == {"groups": 2, "replica": 8, "tensor": 2}


def solution(mesh):
    rows = P(("groups", "replica"), None)
    split = P(("groups", "replica"), "tensor")
    cache = P(("groups", "replica"), None, "tensor")
    placed = (
        rows,
        split,
        cache,
        cache,
        P(None, "tensor"),
        P(None, "tensor"),
        P("replica", "tensor", None),
        P("replica", None, None, "tensor"),
        P("groups"),
        P("groups", None),
        rows,
        rows,
    )
    return jax.shard_map(
        functools.partial(body, layered(mesh)),
        mesh=mesh,
        in_specs=placed,
        out_specs=(split, split, split),
        check_vma=False,
    )
```

```python
import functools

import jax
import jax.numpy as jnp
import numpy as np
from jax import lax
from jax.experimental import pallas as pl
from jax.experimental.pallas import tpu as pltpu
from jax.sharding import PartitionSpec as P

HEAD = 128
GROUP = 8
RANK = 64
REQ = 4
SCALE = 0.5
THETA = 500000.0
LOG2E = 1.4426950408889634
NEG = -1e30
TILE = 64
CHUNK = 1024
PART = 8
ALIGN = 16
VMEM = 60 * 1024 * 1024


def params(*sem):
    return pltpu.CompilerParams(
        dimension_semantics=sem if sem else None, vmem_limit_bytes=VMEM
    )


def nt_dot(a, b):
    return lax.dot_general(a, b, (((1,), (1,)), ((), ())), preferred_element_type=jnp.float32)


def cached_kernel(first, carry_on, info, q_ref, k_ref, v_ref, *rest):
    acc_ref, stat_ref = rest[-2:]
    r = pl.program_id(0) + first
    if carry_on:

        @pl.when(pl.program_id(0) == 0)
        def _():
            acc_ref[...] = rest[0][...]
            stat_ref[...] = rest[1][...]

    rows_all = q_ref.shape[0]
    start = info[0, r]
    count = info[1, r]
    length = info[3, r]
    base0 = (start // ALIGN) * ALIGN
    tiles = (start + count - base0 + TILE - 1) // TILE
    chunks = (length + CHUNK - 1) // CHUNK
    factor = HEAD**-0.5 * LOG2E
    key_iota = lax.broadcasted_iota(jnp.int32, (1, CHUNK), 1)
    row_iota = lax.broadcasted_iota(jnp.int32, (TILE, 128), 0)
    lane = lax.broadcasted_iota(jnp.int32, (TILE, 128), 1)
    many = TILE * PART
    lanes = [slice(i * 128, (i + 1) * 128) for i in range(CHUNK // 128)]

    def tile(t, carry):
        base = pl.multiple_of(jnp.minimum(base0 + t * TILE, rows_all - TILE), ALIGN)
        qt = q_ref[pl.ds(base, TILE), :]
        q = jnp.concatenate([qt[:, h * HEAD : (h + 1) * HEAD] for h in range(PART)], axis=0)

        def chunk(j, state):
            m, l, acc = state
            at = pl.multiple_of(j * CHUNK, CHUNK)
            s = nt_dot(q, k_ref[0, pl.ds(at, CHUNK), :])
            s = s + jnp.where(key_iota + at < length, 0.0, NEG)
            most = s[:, lanes[0]]
            for cut in lanes[1:]:
                most = jnp.maximum(most, s[:, cut])
            top = jnp.maximum(
                m, jnp.broadcast_to(jnp.max(most, axis=1, keepdims=True), (many, 128)) * factor
            )
            alpha = jnp.exp2(m - top)
            l = l * alpha
            weights = []
            for cut in lanes:
                p = jnp.exp2(s[:, cut] * factor - top)
                l = l + p
                weights.append(p.astype(jnp.bfloat16))
            acc = acc * alpha + jnp.dot(
                jnp.concatenate(weights, axis=1),
                v_ref[0, pl.ds(at, CHUNK), :],
                preferred_element_type=jnp.float32,
            )
            return top, l, acc

        m, l, acc = lax.fori_loop(
            0,
            chunks,
            chunk,
            (
                jnp.full((many, 128), NEG, jnp.float32),
                jnp.zeros((many, 128), jnp.float32),
                jnp.zeros((many, HEAD), jnp.float32),
            ),
        )
        l = jnp.sum(l, axis=1, keepdims=True)
        at_row = row_iota + base
        mine = (at_row >= start) & (at_row < start + count)
        rows = pl.ds(base, TILE)
        tops = stat_ref[0, 0, rows, :]
        sums = stat_ref[0, 1, rows, :]
        for h in range(PART):
            part = slice(h * TILE, (h + 1) * TILE)
            columns = slice(h * HEAD, (h + 1) * HEAD)
            acc_ref[0, rows, columns] = jnp.where(mine, acc[part], acc_ref[0, rows, columns])
            here = mine & (lane == h)
            tops = jnp.where(here, m[part], tops)
            sums = jnp.where(here, l[part], sums)
        stat_ref[0, 0, rows, :] = tops
        stat_ref[0, 1, rows, :] = sums
        return carry

    lax.fori_loop(0, tiles, tile, 0)


def cached_attention(info, queries, cache_key, cache_value, step, before):
    part, first = step // 2, step % 2 * (REQ // 2)
    rows = queries.shape[0]
    wide = PART * HEAD
    parts = queries.shape[1] // wide
    head = part * PART // GROUP
    slots = cache_key.shape[1]
    extra = [] if before is None else list(before)
    carry_on = first > 0
    acc_spec = pl.BlockSpec((1, rows, wide), lambda r, s: (part, 0, 0))
    stat_spec = pl.BlockSpec((1, 2, rows, 128), lambda r, s: (part, 0, 0, 0))
    cache = pl.BlockSpec((1, slots, HEAD), lambda r, s: (r + first, 0, head))
    aliased = [acc_spec, stat_spec] if carry_on else [pl.BlockSpec(memory_space=pltpu.HBM)] * 2
    return pl.pallas_call(
        functools.partial(cached_kernel, first, carry_on),
        grid_spec=pltpu.PrefetchScalarGridSpec(
            num_scalar_prefetch=1,
            grid=(REQ // 2,),
            in_specs=[pl.BlockSpec((rows, wide), lambda r, s: (0, part)), cache, cache]
            + (aliased if extra else []),
            out_specs=[acc_spec, stat_spec],
        ),
        out_shape=[
            jax.ShapeDtypeStruct((parts, rows, wide), jnp.float32),
            jax.ShapeDtypeStruct((parts, 2, rows, 128), jnp.float32),
        ],
        input_output_aliases={4: 0, 5: 1} if extra else {},
        compiler_params=params("arbitrary"),
        cost_estimate=pl.CostEstimate(
            flops=4 * rows * wide * 2048,
            bytes_accessed=6 * 1024 * 1024,
            transcendentals=rows * PART * 1024,
        ),
        name="cached_attention",
    )(info, queries, cache_key, cache_value, *extra)


def low_rank_kernel(pick, n_pieces, place, infos, *refs):
    tokens = refs[:4]
    pieces = refs[4 : 4 + n_pieces]
    before = refs[4 + n_pieces : -3]
    outs = refs[-3 - (8 if pick == "early" else 4) : -3]
    token_scr, piece_scr, sems = refs[-3:]
    rows, width = token_scr.shape[1:]
    held = piece_scr.shape[1]
    column = pl.multiple_of(place[2] * width, 128)
    copies = [
        pltpu.make_async_copy(tokens[0].at[:, pl.ds(column, width)], token_scr.at[0], sems.at[0])
    ]
    for n in range(1, 4):
        copies.append(
            pltpu.make_async_copy(tokens[n].at[pl.ds(0, rows)], token_scr.at[n], sems.at[n])
        )
    at = 0
    for p in range(n_pieces):
        if len(pieces[p].shape) == 4:
            target = piece_scr.at[pl.ds(at, pieces[p].shape[0])]
            at += pieces[p].shape[0]
        else:
            target = piece_scr.at[at]
            at += 1
        copies.append(pltpu.make_async_copy(pieces[p], target, sems.at[4 + p]))
    for copy in copies:
        copy.start()
    for n in range(4):
        outs[n][...] = jnp.zeros_like(outs[n]) if pick == "early" else before[n][...]
    for copy in copies:
        copy.wait()
    window = rows // 3 + ALIGN
    row_iota = lax.broadcasted_iota(jnp.int32, (window, 1), 0)
    z, y = place[0], place[1]
    at_end = (z == 0) | (z == 3)

    for n in range(4):

        def one(r, start):
            count = infos[n, r]
            slot = infos[n, REQ + r]
            owner = slot // held
            layer = owner // 2
            other = jnp.where(owner % 2 != y, 1, 0)
            mates = layer // 2 == z // 2
            ends = (layer == 0) | (layer == 3)
            last = at_end & ends & jnp.logical_not(mates)
            if pick == "early":
                kind = jnp.where(at_end, 4, jnp.where(ends, 3, 2))
                kind = jnp.where(mates, jnp.where(layer == z, 0, 1), kind)
                index = kind * 2 + other
                valid = jnp.logical_not(last)
            else:
                index = other
                valid = last

            def product():
                base = pl.multiple_of(
                    jnp.minimum((start // ALIGN) * ALIGN, rows - window), ALIGN
                )
                span = pl.ds(base, window)
                low = jnp.dot(
                    token_scr[n, span, :],
                    piece_scr[index, slot % held, :width, :],
                    preferred_element_type=jnp.float32,
                )
                mine = (row_iota + base >= start) & (row_iota + base < start + count) & valid
                outs[n][span, :] = jnp.where(mine, low, outs[n][span, :])

            if pick == "early":
                product()
                outs[4 + n][r] = jnp.where(
                    last,
                    before[0][other, slot % held],
                    piece_scr[index, slot % held, width:, :],
                )
            else:
                pl.when(valid)(product)
            return start + count

        if pick == "early":
            start = jnp.int32(0)
            for r in range(REQ):
                start = one(r, start)
        else:
            lax.fori_loop(0, REQ, one, 0)


def low_rank_step(pick, place, infos, tokens, pieces, before, width):
    rows = tokens[0].shape[0]
    held, tall, rank = pieces[0].shape[-3:]
    vmem = pl.BlockSpec(memory_space=pltpu.VMEM)
    smem = pl.BlockSpec(memory_space=pltpu.SMEM)
    hbm = pl.BlockSpec(memory_space=pltpu.HBM)
    total = sum(p.shape[0] if p.ndim == 4 else 1 for p in pieces)
    ups = []
    if pick == "early":
        ups = [jax.ShapeDtypeStruct((REQ, tall - width, rank), jnp.bfloat16)] * 4
    return pl.pallas_call(
        functools.partial(low_rank_kernel, pick, len(pieces)),
        in_specs=[smem, smem] + [hbm] * (4 + len(pieces)) + [vmem] * len(before),
        out_specs=[vmem] * (4 + len(ups)),
        out_shape=[jax.ShapeDtypeStruct((rows, rank), jnp.float32)] * 4 + ups,
        scratch_shapes=[
            pltpu.VMEM((4, rows, width), jnp.bfloat16),
            pltpu.VMEM((total, held, tall, rank), jnp.bfloat16),
            pltpu.SemaphoreType.DMA((4 + len(pieces),)),
        ],
        compiler_params=params(),
        cost_estimate=pl.CostEstimate(
            flops=2 * 4 * rows * width * rank * 4, bytes_accessed=6 * 1024 * 1024, transcendentals=0
        ),
        name="low_rank_" + pick,
    )(place, infos, *tokens, *pieces, *before)


def project_kernel(t_ref, k_ref, v_ref, ko_ref, vo_ref):
    t = t_ref[...]
    for w_ref, o_ref in ((k_ref, ko_ref), (v_ref, vo_ref)):
        part = jnp.dot(t, w_ref[...], preferred_element_type=jnp.float32)

        @pl.when(pl.program_id(0) == 0)
        def _():
            o_ref[...] = part

        @pl.when(pl.program_id(0) > 0)
        def _():
            o_ref[...] += part


def project(tokens, key_weight, value_weight):
    rows, width = tokens.shape
    columns = key_weight.shape[1]
    deep = min(width, 2048)
    weight = pl.BlockSpec((deep, columns), lambda i: (i, 0))
    out = pl.BlockSpec((rows, columns), lambda i: (0, 0))
    return pl.pallas_call(
        project_kernel,
        grid=(width // deep,),
        in_specs=[pl.BlockSpec((rows, deep), lambda i: (0, i)), weight, weight],
        out_specs=[out, out],
        out_shape=[jax.ShapeDtypeStruct((rows, columns), jnp.float32)] * 2,
        compiler_params=params("arbitrary"),
        cost_estimate=pl.CostEstimate(
            flops=4 * rows * width * columns, bytes_accessed=16 * 1024 * 1024, transcendentals=0
        ),
        name="project",
    )(tokens, key_weight, value_weight)


def final_kernel(
    info, mine_ref, other_ref, pk_ref, pv_ref, up0, up1, up2, up3, cos_ref, sin_ref, q_ref, acc_ref,
    stat_ref, ctx_ref, ko_ref, vo_ref, up_scr,
):
    rows = q_ref.shape[0]

    @pl.when(pl.program_id(0) % (GROUP // PART) == 0)
    def _():
        low = (mine_ref[...] + other_ref[...]).astype(jnp.bfloat16)
        at_row = lax.broadcasted_iota(jnp.int32, (rows, 1), 0)
        key_lin = pk_ref[...]
        value_lin = pv_ref[...]
        for n, ref in enumerate((up0, up1, up2, up3)):
            up_scr[n] = ref[...]
        tall = RANK // 2
        which = pl.ds(
            pl.multiple_of(pl.program_id(0) // (GROUP // PART) * tall, tall), tall
        )
        for r in range(REQ):
            mine = (at_row >= info[0, r]) & (at_row < info[0, r] + info[1, r])
            up = [up_scr[info[2, c], r, which, :] for c in range(4)]
            up_key = jnp.concatenate(up[:2], axis=0)
            up_value = jnp.concatenate(up[2:], axis=0)
            dk = jnp.dot(low[:, :RANK], up_key, preferred_element_type=jnp.float32)
            dv = jnp.dot(low[:, RANK:], up_value, preferred_element_type=jnp.float32)
            key_lin = key_lin + SCALE * jnp.where(mine, dk, 0.0)
            value_lin = value_lin + SCALE * jnp.where(mine, dv, 0.0)
        turned = key_lin * cos_ref[...] + pltpu.roll(key_lin, HEAD // 2, 1) * sin_ref[...]
        ko_ref[...] = turned.astype(jnp.bfloat16)
        vo_ref[...] = value_lin.astype(jnp.bfloat16)

    factor = HEAD**-0.5 * LOG2E
    most = rows // 3
    span = 2 * most

    def block(b, carry):
        low_key = pl.multiple_of(jnp.maximum(b - 1, 0) * most, most)
        at = pl.multiple_of(b * most, most)
        q_at = lax.broadcasted_iota(jnp.int32, (most, 1), 0) + at
        k_at = lax.broadcasted_iota(jnp.int32, (1, span), 1) + low_key
        q_req = jnp.zeros((most, 1), jnp.int32)
        k_req = jnp.zeros((1, span), jnp.int32)
        for r in range(1, REQ):
            q_req = q_req + (q_at >= info[0, r]).astype(jnp.int32)
            k_req = k_req + (k_at >= info[0, r]).astype(jnp.int32)
        bias = jnp.where((q_req == k_req) & (k_at <= q_at), 0.0, NEG)
        part = pl.ds(at, most)
        lane = lax.broadcasted_iota(jnp.int32, (most, 128), 1)
        heads = [slice(h * HEAD, (h + 1) * HEAD) for h in range(PART)]
        cuts = [slice(h * most, (h + 1) * most) for h in range(PART)]
        q = jnp.concatenate([q_ref[part, h] for h in heads], axis=0)
        scores = nt_dot(q, ko_ref[pl.ds(low_key, span), :])
        fresh_top = jnp.zeros((most, 128), jnp.float32)
        fresh_sum = jnp.ones((most, 128), jnp.float32)
        weights = []
        for h in range(PART):
            s = scores[cuts[h]] * factor + bias
            top = jnp.max(s, axis=1, keepdims=True)
            p = jnp.exp2(s - top)
            fresh_top = jnp.where(lane == h, top, fresh_top)
            fresh_sum = jnp.where(lane == h, jnp.sum(p, axis=1, keepdims=True), fresh_sum)
            weights.append(p.astype(jnp.bfloat16))
        fresh = jnp.dot(
            jnp.concatenate(weights, axis=0),
            vo_ref[pl.ds(low_key, span), :],
            preferred_element_type=jnp.float32,
        )
        live = lane < PART
        before = jnp.where(live, stat_ref[0, 0, part, :], 0.0)
        before_sum = jnp.where(live, stat_ref[0, 1, part, :], 1.0)
        top = jnp.maximum(before, fresh_top)
        old = jnp.exp2(before - top)
        new = jnp.exp2(fresh_top - top)
        total = before_sum * old + fresh_sum * new
        old = old / total
        new = new / total
        for h in range(PART):
            out = (
                acc_ref[0, part, heads[h]] * old[:, h : h + 1]
                + fresh[cuts[h]] * new[:, h : h + 1]
            )
            ctx_ref[part, heads[h]] = out.astype(jnp.bfloat16)
        return carry

    lax.fori_loop(0, 3, block, 0)


def final_step(info, mine, other, pk, pv, ups, cosine, sine, queries, acc, stat):
    rows = queries.shape[0]
    wide = PART * HEAD
    parts = queries.shape[1] // wide
    each = GROUP // PART
    heads = parts // each
    rank2 = mine.shape[1]
    whole = lambda shape: pl.BlockSpec(shape, lambda i, s: (0,) * len(shape))
    of_head = pl.BlockSpec((rows, HEAD), lambda i, s: (0, i // each))
    return pl.pallas_call(
        final_kernel,
        grid_spec=pltpu.PrefetchScalarGridSpec(
            num_scalar_prefetch=1,
            grid=(parts,),
            in_specs=[
                whole((rows, rank2)),
                whole((rows, rank2)),
                of_head,
                of_head,
                *([whole(ups[0].shape)] * 4),
                whole((rows, HEAD)),
                whole((rows, HEAD)),
                pl.BlockSpec((rows, wide), lambda i, s: (0, i)),
                pl.BlockSpec((1, rows, wide), lambda i, s: (i, 0, 0)),
                pl.BlockSpec((1, 2, rows, 128), lambda i, s: (i, 0, 0, 0)),
            ],
            out_specs=[pl.BlockSpec((rows, wide), lambda i, s: (0, i)), of_head, of_head],
            scratch_shapes=[pltpu.VMEM((4, *ups[0].shape), jnp.bfloat16)],
        ),
        out_shape=[
            jax.ShapeDtypeStruct(queries.shape, jnp.bfloat16),
            jax.ShapeDtypeStruct((rows, heads * HEAD), jnp.bfloat16),
            jax.ShapeDtypeStruct((rows, heads * HEAD), jnp.bfloat16),
        ],
        compiler_params=params("arbitrary"),
        name="final_step",
    )(info, mine, other, pk, pv, *ups, cosine, sine, queries, acc, stat)


def after(value, *others):
    return lax.optimization_barrier((value, *others))[0]


def body(
    fast,
    tokens,
    queries,
    stored_key_cache,
    stored_value_cache,
    key_weight_matrix,
    value_weight_matrix,
    adapter_down_weight,
    adapter_up_weight,
    adapter_slot_index,
    request_adapter_index,
    fresh_token_count,
    cache_token_length,
):
    group = lax.axis_index("groups")
    replica = lax.axis_index("replica")
    core = lax.axis_index("tensor")
    rows, width = tokens.shape
    held, half, rank2 = adapter_down_weight.shape
    counts = fresh_token_count[0]
    lengths = cache_token_length[0]
    order = jnp.arange(REQ, dtype=jnp.int32)
    starts = jnp.sum(jnp.where(order[:, None] > order[None, :], counts[None, :], 0), axis=1)
    wanted = lax.dynamic_index_in_dim(request_adapter_index, replica, 0, False)
    n_slots = adapter_slot_index.shape[0]
    slots = jnp.sum(
        jnp.where(
            wanted[:, None] == jnp.arange(n_slots, dtype=jnp.int32)[None, :],
            adapter_slot_index[None, :],
            0,
        ),
        axis=1,
    )
    here = group * 2 + replica % 2 if fast else 0
    info = jnp.stack([starts, counts, order ^ here, lengths]).astype(jnp.int32)

    at_row = jnp.arange(rows, dtype=jnp.int32)
    of_request = jnp.sum(at_row[:, None] >= starts[None, 1:], axis=1)
    shift = lengths - starts
    position = at_row + jnp.sum(
        jnp.where(of_request[:, None] == jnp.arange(REQ)[None, :], shift[None, :], 0), axis=1
    )
    frequency = THETA ** (-(jnp.arange(HEAD // 2, dtype=jnp.float32) * 2.0) / HEAD)
    angles = position.astype(jnp.float32)[:, None] * frequency
    cosine = jnp.cos(angles)
    sine = jnp.sin(angles)
    cosine = jnp.concatenate([cosine, cosine], axis=1)
    sine = jnp.concatenate([-sine, sine], axis=1)

    n_replica = lax.axis_size("replica")
    tall = RANK // 2

    if fast:
        y = replica % 2
        column = group * 2 + y
        quarter = half // 4
        by_x = lambda a: lax.ppermute(a, "groups", [(0, 1), (1, 0)])
        by_y = lambda a: lax.ppermute(a, "replica", [(r, r ^ 1) for r in range(n_replica)])
        by_xy = lambda a: lax.ppermute(
            a,
            ("groups", "replica"),
            [
                (g * n_replica + r, (1 - g) * n_replica + (r ^ 1))
                for g in range(2)
                for r in range(n_replica)
            ],
        )
        mesh_z = lambda a, pairs: lax.ppermute(
            a, "replica", [(2 * f + p, 2 * t + p) for f, t in pairs for p in range(2)]
        )
        in_pair = lambda a: mesh_z(a, [(0, 1), (1, 0), (2, 3), (3, 2)])
        across = lambda a: mesh_z(a, [(1, 2), (2, 1)])
        outward = lambda a: mesh_z(a, [(1, 0), (2, 3)])

        def factor_part(c):
            down = lax.dynamic_slice_in_dim(adapter_down_weight, c * quarter, quarter, 1)
            up = lax.dynamic_slice(
                adapter_up_weight,
                (0, c // 2, (c % 2) * tall, 0),
                (held, 1, tall, adapter_up_weight.shape[3]),
            )[:, 0]
            return jnp.concatenate([down, up[:, :, :HEAD], up[:, :, HEAD:]], axis=1)

        own_b = by_y(factor_part(column ^ 1))
        own_a = factor_part(column)
        pair_a = in_pair(own_a)
        mid_a = across(own_a)
        note = jnp.concatenate([counts, slots])
        below = jnp.pad(note.astype(jnp.bfloat16)[None, :], ((0, 15), (0, quarter - 2 * REQ)))
        token_part = lambda c, t: jnp.concatenate(
            [lax.dynamic_slice_in_dim(t, core * half + c * quarter, quarter, 1), below]
        )
        t_x = by_x(token_part(column ^ 2, tokens))
        tokens_later = after(tokens, own_b)
        t_y = by_y(token_part(column ^ 1, tokens_later))
        t_d = by_xy(token_part(column ^ 3, tokens_later))
        plain_key, plain_value = project(tokens, key_weight_matrix, value_weight_matrix)
        far_up = mesh_z(jnp.stack([own_a[:, quarter:], own_b[:, quarter:]]), [(0, 3), (3, 0)])
        own_b = after(own_b, plain_key)
        pair_b = in_pair(own_b)
        mid_b = across(own_b)
        part = lambda n, q, b: cached_attention(
            info, q, stored_key_cache, stored_value_cache, n, b
        )
        cached = part(0, after(queries, own_b), None)
        across_2 = across(after(jnp.stack([pair_a, pair_b]), cached[0]))
        outward_2 = outward(after(jnp.stack([mid_a, mid_b]), cached[0]))
        cached = part(1, after(queries, pair_b, mid_b, far_up), cached)
        cached = part(2, queries, cached)
        outward_3 = outward(after(across_2, cached[0]))
        place = jnp.stack([replica // 2, y, core * 4 + column]).astype(jnp.int32)
        infos = jnp.stack(
            [note] + [t[rows, : 2 * REQ].astype(jnp.int32) for t in (t_y, t_x, t_d)]
        )
        layer_tokens = [tokens, t_y, t_x, t_d]
        early = [own_a, own_b, pair_a, pair_b, mid_a, mid_b, across_2, outward_2]
        low = low_rank_step(
            "early", after(place, cached[0]), infos, layer_tokens, early, [far_up], quarter
        )
        ups = [low[4], by_y(low[5]), by_x(low[6]), by_xy(low[7])]
        cached = part(3, after(queries, low[0]), cached)
        outward_3 = after(outward_3, cached[0], *ups)
        low = low_rank_step("late", place, infos, layer_tokens, [outward_3], low[:4], quarter)
        low_sum = low[0] + by_y(low[1]) + by_x(low[2]) + by_xy(low[3])
    else:
        down_all = lax.all_gather(adapter_down_weight, "replica", axis=0, tiled=True)
        mine = lax.dynamic_slice_in_dim(tokens, core * half, half, 1)
        low_sum = jnp.zeros((rows, rank2), jnp.float32)
        for r in range(REQ):
            low_sum = low_sum + jnp.where(
                (of_request == r)[:, None],
                jnp.dot(mine, down_all[slots[r]], preferred_element_type=jnp.float32),
                0.0,
            )
        up_all = lax.all_gather(adapter_up_weight, "replica", axis=0, tiled=True)[slots]
        ups = []
        for c in range(4):
            up = up_all[:, c // 2, (c % 2) * tall : (c % 2 + 1) * tall]
            ups.append(jnp.concatenate([up[:, :, :HEAD], up[:, :, HEAD:]], axis=1))
        plain_key, plain_value = project(tokens, key_weight_matrix, value_weight_matrix)
        cached = None
        for n in range(2 * queries.shape[1] // (PART * HEAD)):
            cached = cached_attention(
                info, queries, stored_key_cache, stored_value_cache, n, cached
            )
    low_other = lax.ppermute(low_sum, "tensor", [(0, 1), (1, 0)])
    return tuple(
        final_step(
            info, low_sum, low_other, plain_key, plain_value, ups, cosine, sine, queries, *cached
        )
    )


def layered(mesh):
    return dict(mesh.shape) == {"groups": 2, "replica": 8, "tensor": 2}


def solution(mesh):
    rows = P(("groups", "replica"), None)
    split = P(("groups", "replica"), "tensor")
    cache = P(("groups", "replica"), None, "tensor")
    placed = (
        rows,
        split,
        cache,
        cache,
        P(None, "tensor"),
        P(None, "tensor"),
        P("replica", "tensor", None),
        P("replica", None, None, "tensor"),
        P("groups"),
        P("groups", None),
        rows,
        rows,
    )
    return jax.shard_map(
        functools.partial(body, layered(mesh)),
        mesh=mesh,
        in_specs=placed,
        out_specs=(split, split, split),
        check_vma=False,
    )
```

```python
import functools

import jax
import jax.numpy as jnp
import numpy as np
from jax import lax
from jax.experimental import pallas as pl
from jax.experimental.pallas import tpu as pltpu
from jax.sharding import PartitionSpec as P

HEAD = 128
GROUP = 8
RANK = 64
REQ = 4
SCALE = 0.5
THETA = 500000.0
LOG2E = 1.4426950408889634
NEG = -1e30
TILE = 32
CHUNK = 512
PART = 8
ALIGN = 16
VMEM = 60 * 1024 * 1024


def params(*sem, vmem=VMEM):
    return pltpu.CompilerParams(
        dimension_semantics=sem if sem else None, vmem_limit_bytes=vmem
    )


def nt_dot(a, b):
    return lax.dot_general(a, b, (((1,), (1,)), ((), ())), preferred_element_type=jnp.float32)


def cached_kernel(info, q_ref, k_ref, v_ref, *rest):
    acc_ref, stat_ref = rest[-2:]
    r = pl.program_id(0)
    rows_all = q_ref.shape[0]
    start = info[0, r]
    count = info[1, r]
    length = info[3, r]
    base0 = (start // ALIGN) * ALIGN
    tiles = (start + count - base0 + TILE - 1) // TILE
    units = (length + CHUNK - 1) // CHUNK
    factor = HEAD**-0.5 * LOG2E
    row_iota = lax.broadcasted_iota(jnp.int32, (TILE, 128), 0)
    lane = lax.broadcasted_iota(jnp.int32, (TILE, 128), 1)
    many = TILE * PART

    def tile(width, t, carry):
        base = pl.multiple_of(jnp.minimum(base0 + t * TILE, rows_all - TILE), ALIGN)
        qt = q_ref[pl.ds(base, TILE), :]
        q = jnp.concatenate([qt[:, h * HEAD : (h + 1) * HEAD] for h in range(PART)], axis=0)
        lanes = [slice(i * 128, (i + 1) * 128) for i in range(width // 128)]
        key_iota = lax.broadcasted_iota(jnp.int32, (1, width), 1)
        s = nt_dot(q, k_ref[0, :width, :]) + jnp.where(key_iota < length, 0.0, NEG)
        most = s[:, lanes[0]]
        for cut in lanes[1:]:
            most = jnp.maximum(most, s[:, cut])
        m = jnp.broadcast_to(jnp.max(most, axis=1, keepdims=True), (many, 128)) * factor
        l = jnp.zeros((many, 128), jnp.float32)
        weights = []
        for cut in lanes:
            p = jnp.exp2(s[:, cut] * factor - m)
            l = l + p
            weights.append(p.astype(jnp.bfloat16))
        acc = jnp.dot(
            jnp.concatenate(weights, axis=1),
            v_ref[0, :width, :],
            preferred_element_type=jnp.float32,
        )
        l = jnp.sum(l, axis=1, keepdims=True)
        at_row = row_iota + base
        mine = (at_row >= start) & (at_row < start + count)
        rows = pl.ds(base, TILE)
        tops = stat_ref[0, 0, rows, :]
        sums = stat_ref[0, 1, rows, :]
        for h in range(PART):
            part = slice(h * TILE, (h + 1) * TILE)
            columns = slice(h * HEAD, (h + 1) * HEAD)
            acc_ref[0, rows, columns] = jnp.where(mine, acc[part], acc_ref[0, rows, columns])
            here = mine & (lane == h)
            tops = jnp.where(here, m[part], tops)
            sums = jnp.where(here, l[part], sums)
        stat_ref[0, 0, rows, :] = tops
        stat_ref[0, 1, rows, :] = sums
        return carry

    for n in range(1, k_ref.shape[1] // CHUNK + 1):

        @pl.when(units == n)
        def _():
            lax.fori_loop(0, tiles, functools.partial(tile, n * CHUNK), 0)


def cached_attention(info, queries, cache_key, cache_value, part, before):
    rows = queries.shape[0]
    wide = PART * HEAD
    parts = queries.shape[1] // wide
    head = part * PART // GROUP
    slots = cache_key.shape[1]
    extra = [] if before is None else list(before)
    acc_spec = pl.BlockSpec((1, rows, wide), lambda r, s: (part, 0, 0))
    stat_spec = pl.BlockSpec((1, 2, rows, 128), lambda r, s: (part, 0, 0, 0))
    cache = pl.BlockSpec((1, slots, HEAD), lambda r, s: (r, 0, head))
    return pl.pallas_call(
        cached_kernel,
        grid_spec=pltpu.PrefetchScalarGridSpec(
            num_scalar_prefetch=1,
            grid=(REQ,),
            in_specs=[pl.BlockSpec((rows, wide), lambda r, s: (0, part)), cache, cache]
            + [pl.BlockSpec(memory_space=pltpu.HBM)] * len(extra),
            out_specs=[acc_spec, stat_spec],
        ),
        out_shape=[
            jax.ShapeDtypeStruct((parts, rows, wide), jnp.float32),
            jax.ShapeDtypeStruct((parts, 2, rows, 128), jnp.float32),
        ],
        input_output_aliases={4: 0, 5: 1} if extra else {},
        compiler_params=params("arbitrary"),
        cost_estimate=pl.CostEstimate(
            flops=4 * rows * wide * 4096,
            bytes_accessed=6 * 1024 * 1024,
            transcendentals=rows * PART * 2048,
        ),
        name="cached_attention",
    )(info, queries, cache_key, cache_value, *extra)


def low_rank_kernel(pick, n_pieces, place, infos, *refs):
    tokens = refs[:4]
    pieces = refs[4 : 4 + n_pieces]
    before = refs[4 + n_pieces : -3]
    outs = refs[-3 - (8 if pick == "early" else 4) : -3]
    token_scr, piece_scr, sems = refs[-3:]
    rows, width = token_scr.shape[1:]
    held = piece_scr.shape[1]
    column = pl.multiple_of(place[2] * width, 128)
    copies = [
        pltpu.make_async_copy(tokens[0].at[:, pl.ds(column, width)], token_scr.at[0], sems.at[0])
    ]
    for n in range(1, 4):
        copies.append(
            pltpu.make_async_copy(tokens[n].at[pl.ds(0, rows)], token_scr.at[n], sems.at[n])
        )
    at = 0
    for p in range(n_pieces):
        if len(pieces[p].shape) == 4:
            target = piece_scr.at[pl.ds(at, pieces[p].shape[0])]
            at += pieces[p].shape[0]
        else:
            target = piece_scr.at[at]
            at += 1
        copies.append(pltpu.make_async_copy(pieces[p], target, sems.at[4 + p]))
    for copy in copies:
        copy.start()
    for n in range(4):
        outs[n][...] = jnp.zeros_like(outs[n]) if pick == "early" else before[n][...]
    for copy in copies:
        copy.wait()
    window = rows // 3 + ALIGN
    row_iota = lax.broadcasted_iota(jnp.int32, (window, 1), 0)
    z, y = place[0], place[1]
    at_end = (z == 0) | (z == 3)

    for n in range(4):

        def one(r, start):
            count = infos[n, r]
            slot = infos[n, REQ + r]
            owner = slot // held
            layer = owner // 2
            other = jnp.where(owner % 2 != y, 1, 0)
            mates = layer // 2 == z // 2
            ends = (layer == 0) | (layer == 3)
            last = at_end & ends & jnp.logical_not(mates)
            if pick == "early":
                kind = jnp.where(at_end, 4, jnp.where(ends, 3, 2))
                kind = jnp.where(mates, jnp.where(layer == z, 0, 1), kind)
                index = kind * 2 + other
                valid = jnp.logical_not(last)
            else:
                index = other
                valid = last

            def product():
                base = pl.multiple_of(
                    jnp.minimum((start // ALIGN) * ALIGN, rows - window), ALIGN
                )
                span = pl.ds(base, window)
                low = jnp.dot(
                    token_scr[n, span, :],
                    piece_scr[index, slot % held, :width, :],
                    preferred_element_type=jnp.float32,
                )
                mine = (row_iota + base >= start) & (row_iota + base < start + count) & valid
                outs[n][span, :] = jnp.where(mine, low, outs[n][span, :])

            if pick == "early":
                product()
                outs[4 + n][r] = jnp.where(
                    last,
                    before[0][other, slot % held],
                    piece_scr[index, slot % held, width:, :],
                )
            else:
                pl.when(valid)(product)
            return start + count

        if pick == "early":
            start = jnp.int32(0)
            for r in range(REQ):
                start = one(r, start)
        else:
            lax.fori_loop(0, REQ, one, 0)


def low_rank_step(pick, place, infos, tokens, pieces, before, width):
    rows = tokens[0].shape[0]
    held, tall, rank = pieces[0].shape[-3:]
    vmem = pl.BlockSpec(memory_space=pltpu.VMEM)
    smem = pl.BlockSpec(memory_space=pltpu.SMEM)
    hbm = pl.BlockSpec(memory_space=pltpu.HBM)
    total = sum(p.shape[0] if p.ndim == 4 else 1 for p in pieces)
    ups = []
    if pick == "early":
        ups = [jax.ShapeDtypeStruct((REQ, tall - width, rank), jnp.bfloat16)] * 4
    return pl.pallas_call(
        functools.partial(low_rank_kernel, pick, len(pieces)),
        in_specs=[smem, smem] + [hbm] * (4 + len(pieces)) + [vmem] * len(before),
        out_specs=[vmem] * (4 + len(ups)),
        out_shape=[jax.ShapeDtypeStruct((rows, rank), jnp.float32)] * 4 + ups,
        scratch_shapes=[
            pltpu.VMEM((4, rows, width), jnp.bfloat16),
            pltpu.VMEM((total, held, tall, rank), jnp.bfloat16),
            pltpu.SemaphoreType.DMA((4 + len(pieces),)),
        ],
        compiler_params=params(),
        cost_estimate=pl.CostEstimate(
            flops=2 * 4 * rows * width * rank * 4, bytes_accessed=6 * 1024 * 1024, transcendentals=0
        ),
        name="low_rank_" + pick,
    )(place, infos, *tokens, *pieces, *before)


def final_kernel(
    info, mine_ref, other_ref, pk_ref, pv_ref, up0, up1, up2, up3, cos_ref, sin_ref, q_ref, acc_ref,
    stat_ref, ctx_ref, ko_ref, vo_ref, up_scr,
):
    rows = q_ref.shape[0]

    @pl.when(pl.program_id(0) % (GROUP // PART) == 0)
    def _():
        low = (mine_ref[...] + other_ref[...]).astype(jnp.bfloat16)
        at_row = lax.broadcasted_iota(jnp.int32, (rows, 1), 0)
        key_lin = pk_ref[...]
        value_lin = pv_ref[...]
        for n, ref in enumerate((up0, up1, up2, up3)):
            up_scr[n] = ref[...]
        tall = RANK // 2
        which = pl.ds(
            pl.multiple_of(pl.program_id(0) // (GROUP // PART) * tall, tall), tall
        )
        for r in range(REQ):
            mine = (at_row >= info[0, r]) & (at_row < info[0, r] + info[1, r])
            up = [up_scr[info[2, c], r, which, :] for c in range(4)]
            up_key = jnp.concatenate(up[:2], axis=0)
            up_value = jnp.concatenate(up[2:], axis=0)
            dk = jnp.dot(low[:, :RANK], up_key, preferred_element_type=jnp.float32)
            dv = jnp.dot(low[:, RANK:], up_value, preferred_element_type=jnp.float32)
            key_lin = key_lin + SCALE * jnp.where(mine, dk, 0.0)
            value_lin = value_lin + SCALE * jnp.where(mine, dv, 0.0)
        turned = key_lin * cos_ref[...] + pltpu.roll(key_lin, HEAD // 2, 1) * sin_ref[...]
        ko_ref[...] = turned.astype(jnp.bfloat16)
        vo_ref[...] = value_lin.astype(jnp.bfloat16)

    factor = HEAD**-0.5 * LOG2E
    most = rows // 3
    span = 2 * most

    def block(b, carry):
        low_key = pl.multiple_of(jnp.maximum(b - 1, 0) * most, most)
        at = pl.multiple_of(b * most, most)
        q_at = lax.broadcasted_iota(jnp.int32, (most, 1), 0) + at
        k_at = lax.broadcasted_iota(jnp.int32, (1, span), 1) + low_key
        q_req = jnp.zeros((most, 1), jnp.int32)
        k_req = jnp.zeros((1, span), jnp.int32)
        for r in range(1, REQ):
            q_req = q_req + (q_at >= info[0, r]).astype(jnp.int32)
            k_req = k_req + (k_at >= info[0, r]).astype(jnp.int32)
        bias = jnp.where((q_req == k_req) & (k_at <= q_at), 0.0, NEG)
        part = pl.ds(at, most)
        lane = lax.broadcasted_iota(jnp.int32, (most, 128), 1)
        heads = [slice(h * HEAD, (h + 1) * HEAD) for h in range(PART)]
        cuts = [slice(h * most, (h + 1) * most) for h in range(PART)]
        q = jnp.concatenate([q_ref[part, h] for h in heads], axis=0)
        scores = nt_dot(q, ko_ref[pl.ds(low_key, span), :])
        fresh_top = jnp.zeros((most, 128), jnp.float32)
        fresh_sum = jnp.ones((most, 128), jnp.float32)
        weights = []
        for h in range(PART):
            s = scores[cuts[h]] * factor + bias
            top = jnp.max(s, axis=1, keepdims=True)
            p = jnp.exp2(s - top)
            fresh_top = jnp.where(lane == h, top, fresh_top)
            fresh_sum = jnp.where(lane == h, jnp.sum(p, axis=1, keepdims=True), fresh_sum)
            weights.append(p.astype(jnp.bfloat16))
        fresh = jnp.dot(
            jnp.concatenate(weights, axis=0),
            vo_ref[pl.ds(low_key, span), :],
            preferred_element_type=jnp.float32,
        )
        live = lane < PART
        before = jnp.where(live, stat_ref[0, 0, part, :], 0.0)
        before_sum = jnp.where(live, stat_ref[0, 1, part, :], 1.0)
        top = jnp.maximum(before, fresh_top)
        old = jnp.exp2(before - top)
        new = jnp.exp2(fresh_top - top)
        total = before_sum * old + fresh_sum * new
        old = old / total
        new = new / total
        for h in range(PART):
            out = (
                acc_ref[0, part, heads[h]] * old[:, h : h + 1]
                + fresh[cuts[h]] * new[:, h : h + 1]
            )
            ctx_ref[part, heads[h]] = out.astype(jnp.bfloat16)
        return carry

    lax.fori_loop(0, 3, block, 0)


def final_step(info, mine, other, pk, pv, ups, cosine, sine, queries, acc, stat):
    rows = queries.shape[0]
    wide = PART * HEAD
    parts = queries.shape[1] // wide
    each = GROUP // PART
    heads = parts // each
    rank2 = mine.shape[1]
    whole = lambda shape: pl.BlockSpec(shape, lambda i, s: (0,) * len(shape))
    of_head = pl.BlockSpec((rows, HEAD), lambda i, s: (0, i // each))
    return pl.pallas_call(
        final_kernel,
        grid_spec=pltpu.PrefetchScalarGridSpec(
            num_scalar_prefetch=1,
            grid=(parts,),
            in_specs=[
                whole((rows, rank2)),
                whole((rows, rank2)),
                of_head,
                of_head,
                *([whole(ups[0].shape)] * 4),
                whole((rows, HEAD)),
                whole((rows, HEAD)),
                pl.BlockSpec((rows, wide), lambda i, s: (0, i)),
                pl.BlockSpec((1, rows, wide), lambda i, s: (i, 0, 0)),
                pl.BlockSpec((1, 2, rows, 128), lambda i, s: (i, 0, 0, 0)),
            ],
            out_specs=[pl.BlockSpec((rows, wide), lambda i, s: (0, i)), of_head, of_head],
            scratch_shapes=[pltpu.VMEM((4, *ups[0].shape), jnp.bfloat16)],
        ),
        out_shape=[
            jax.ShapeDtypeStruct(queries.shape, jnp.bfloat16),
            jax.ShapeDtypeStruct((rows, heads * HEAD), jnp.bfloat16),
            jax.ShapeDtypeStruct((rows, heads * HEAD), jnp.bfloat16),
        ],
        compiler_params=params("arbitrary", vmem=VMEM // 2),
        name="final_step",
    )(info, mine, other, pk, pv, *ups, cosine, sine, queries, acc, stat)


def after(value, *others):
    return lax.optimization_barrier((value, *others))[0]


def body(
    fast,
    tokens,
    queries,
    stored_key_cache,
    stored_value_cache,
    key_weight_matrix,
    value_weight_matrix,
    adapter_down_weight,
    adapter_up_weight,
    adapter_slot_index,
    request_adapter_index,
    fresh_token_count,
    cache_token_length,
):
    group = lax.axis_index("groups")
    replica = lax.axis_index("replica")
    core = lax.axis_index("tensor")
    rows, width = tokens.shape
    held, half, rank2 = adapter_down_weight.shape
    counts = fresh_token_count[0]
    lengths = cache_token_length[0]
    order = jnp.arange(REQ, dtype=jnp.int32)
    starts = jnp.sum(jnp.where(order[:, None] > order[None, :], counts[None, :], 0), axis=1)
    wanted = lax.dynamic_index_in_dim(request_adapter_index, replica, 0, False)
    n_slots = adapter_slot_index.shape[0]
    slots = jnp.sum(
        jnp.where(
            wanted[:, None] == jnp.arange(n_slots, dtype=jnp.int32)[None, :],
            adapter_slot_index[None, :],
            0,
        ),
        axis=1,
    )
    here = group * 2 + replica % 2 if fast else 0
    info = jnp.stack([starts, counts, order ^ here, lengths]).astype(jnp.int32)

    at_row = jnp.arange(rows, dtype=jnp.int32)
    of_request = jnp.sum(at_row[:, None] >= starts[None, 1:], axis=1)
    shift = lengths - starts
    position = at_row + jnp.sum(
        jnp.where(of_request[:, None] == jnp.arange(REQ)[None, :], shift[None, :], 0), axis=1
    )
    frequency = THETA ** (-(jnp.arange(HEAD // 2, dtype=jnp.float32) * 2.0) / HEAD)
    angles = position.astype(jnp.float32)[:, None] * frequency
    cosine = jnp.cos(angles)
    sine = jnp.sin(angles)
    cosine = jnp.concatenate([cosine, cosine], axis=1)
    sine = jnp.concatenate([-sine, sine], axis=1)

    n_replica = lax.axis_size("replica")
    tall = RANK // 2

    if fast:
        y = replica % 2
        column = group * 2 + y
        quarter = half // 4
        by_x = lambda a: lax.ppermute(a, "groups", [(0, 1), (1, 0)])
        by_y = lambda a: lax.ppermute(a, "replica", [(r, r ^ 1) for r in range(n_replica)])
        by_xy = lambda a: lax.ppermute(
            a,
            ("groups", "replica"),
            [
                (g * n_replica + r, (1 - g) * n_replica + (r ^ 1))
                for g in range(2)
                for r in range(n_replica)
            ],
        )
        mesh_z = lambda a, pairs: lax.ppermute(
            a, "replica", [(2 * f + p, 2 * t + p) for f, t in pairs for p in range(2)]
        )
        in_pair = lambda a: mesh_z(a, [(0, 1), (1, 0), (2, 3), (3, 2)])
        across = lambda a: mesh_z(a, [(1, 2), (2, 1)])
        outward = lambda a: mesh_z(a, [(1, 0), (2, 3)])

        def factor_part(c, factors):
            down = lax.dynamic_slice_in_dim(factors, c * quarter, quarter, 1)
            up = lax.dynamic_slice(
                adapter_up_weight,
                (0, c // 2, (c % 2) * tall, 0),
                (held, 1, tall, adapter_up_weight.shape[3]),
            )[:, 0]
            return jnp.concatenate([down, up[:, :, :HEAD], up[:, :, HEAD:]], axis=1)

        to_mate = factor_part(column ^ 1, adapter_down_weight)
        own_b = by_y(to_mate)
        own_a = factor_part(column, after(adapter_down_weight, to_mate))
        pair_a = in_pair(own_a)
        mid_a = across(own_a)
        note = jnp.concatenate([counts, slots])
        below = jnp.pad(note.astype(jnp.bfloat16)[None, :], ((0, 15), (0, quarter - 2 * REQ)))
        token_part = lambda c: jnp.concatenate(
            [lax.dynamic_slice_in_dim(tokens, core * half + c * quarter, quarter, 1), below]
        )
        for_x, for_y, for_d = (token_part(column ^ c) for c in (2, 1, 3))
        t_x = by_x(for_x)
        own_b, for_y, for_d = lax.optimization_barrier((own_b, for_y, for_d))
        t_y = by_y(for_y)
        t_d = by_xy(for_d)
        tokens_later = after(tokens, own_b)
        far_up = mesh_z(jnp.stack([own_a[:, quarter:], own_b[:, quarter:]]), [(0, 3), (3, 0)])
        pair_b = in_pair(own_b)
        mid_b = across(own_b)
        plain_key = jnp.dot(tokens_later, key_weight_matrix, preferred_element_type=jnp.float32)
        part = lambda n, q, b: cached_attention(
            info, q, stored_key_cache, stored_value_cache, n, b
        )
        across_2 = across(after(jnp.stack([pair_a, pair_b]), plain_key))
        outward_2 = outward(after(jnp.stack([mid_a, mid_b]), plain_key))
        cached = part(0, after(queries, pair_b, mid_b, far_up, t_x, plain_key), None)
        outward_3 = outward(after(across_2, cached[0]))
        plain_value = jnp.dot(
            after(tokens, cached[0]), value_weight_matrix, preferred_element_type=jnp.float32
        )
        place = jnp.stack([replica // 2, y, core * 4 + column]).astype(jnp.int32)
        t_y, t_x, t_d, _ = lax.optimization_barrier((t_y, t_x, t_d, plain_value))
        infos = jnp.stack(
            [note] + [t[rows, : 2 * REQ].astype(jnp.int32) for t in (t_y, t_x, t_d)]
        )
        layer_tokens = [tokens, t_y, t_x, t_d]
        early = [own_a, own_b, pair_a, pair_b, mid_a, mid_b, across_2, outward_2]
        low = low_rank_step("early", place, infos, layer_tokens, early, [far_up], quarter)
        ups = [low[4], by_y(low[5]), by_x(low[6]), by_xy(low[7])]
        cached = part(1, after(queries, low[0]), cached)
        outward_3 = after(outward_3, cached[0], *ups)
        low = low_rank_step("late", place, infos, layer_tokens, [outward_3], low[:4], quarter)
        low_sum = low[0] + by_y(low[1]) + by_x(low[2]) + by_xy(low[3])
    else:
        down_all = lax.all_gather(adapter_down_weight, "replica", axis=0, tiled=True)
        mine = lax.dynamic_slice_in_dim(tokens, core * half, half, 1)
        low_sum = jnp.zeros((rows, rank2), jnp.float32)
        for r in range(REQ):
            low_sum = low_sum + jnp.where(
                (of_request == r)[:, None],
                jnp.dot(mine, down_all[slots[r]], preferred_element_type=jnp.float32),
                0.0,
            )
        up_all = lax.all_gather(adapter_up_weight, "replica", axis=0, tiled=True)[slots]
        ups = []
        for c in range(4):
            up = up_all[:, c // 2, (c % 2) * tall : (c % 2 + 1) * tall]
            ups.append(jnp.concatenate([up[:, :, :HEAD], up[:, :, HEAD:]], axis=1))
        plain_key = jnp.dot(tokens, key_weight_matrix, preferred_element_type=jnp.float32)
        plain_value = jnp.dot(tokens, value_weight_matrix, preferred_element_type=jnp.float32)
        cached = None
        for n in range(queries.shape[1] // (PART * HEAD)):
            cached = cached_attention(
                info, queries, stored_key_cache, stored_value_cache, n, cached
            )
    low_other = lax.ppermute(low_sum, "tensor", [(0, 1), (1, 0)])
    return tuple(
        final_step(
            info, low_sum, low_other, plain_key, plain_value, ups, cosine, sine, queries, *cached
        )
    )


def layered(mesh):
    return dict(mesh.shape) == {"groups": 2, "replica": 8, "tensor": 2}


def solution(mesh):
    rows = P(("groups", "replica"), None)
    split = P(("groups", "replica"), "tensor")
    cache = P(("groups", "replica"), None, "tensor")
    placed = (
        rows,
        split,
        cache,
        cache,
        P(None, "tensor"),
        P(None, "tensor"),
        P("replica", "tensor", None),
        P("replica", None, None, "tensor"),
        P("groups"),
        P("groups", None),
        rows,
        rows,
    )
    return jax.shard_map(
        functools.partial(body, layered(mesh)),
        mesh=mesh,
        in_specs=placed,
        out_specs=(split, split, split),
        check_vma=False,
    )
```

```python
import functools

import jax
import jax.numpy as jnp
import numpy as np
from jax import lax
from jax.experimental import pallas as pl
from jax.experimental.pallas import tpu as pltpu
from jax.sharding import PartitionSpec as P

HEAD = 128
GROUP = 8
RANK = 64
REQ = 4
SCALE = 0.5
THETA = 500000.0
LOG2E = 1.4426950408889634
NEG = -1e30
TILE = 32
CHUNK = 512
PART = 8
ALIGN = 16
VMEM = 60 * 1024 * 1024


def params(*sem, vmem=VMEM):
    return pltpu.CompilerParams(
        dimension_semantics=sem if sem else None, vmem_limit_bytes=vmem
    )


def nt_dot(a, b):
    return lax.dot_general(a, b, (((1,), (1,)), ((), ())), preferred_element_type=jnp.float32)


def cached_kernel(first, carry_on, info, q_ref, k_ref, v_ref, *rest):
    acc_ref, stat_ref = rest[-2:]
    r = pl.program_id(0) + first
    if carry_on:

        @pl.when(pl.program_id(0) == 0)
        def _():
            acc_ref[...] = rest[0][...]
            stat_ref[...] = rest[1][...]

    rows_all = q_ref.shape[0]
    start = info[0, r]
    count = info[1, r]
    length = info[3, r]
    base0 = (start // ALIGN) * ALIGN
    tiles = (start + count - base0 + TILE - 1) // TILE
    units = (length + CHUNK - 1) // CHUNK
    factor = HEAD**-0.5 * LOG2E
    row_iota = lax.broadcasted_iota(jnp.int32, (TILE, 128), 0)
    lane = lax.broadcasted_iota(jnp.int32, (TILE, 128), 1)
    many = TILE * PART

    def tile(width, t, carry):
        base = pl.multiple_of(jnp.minimum(base0 + t * TILE, rows_all - TILE), ALIGN)
        qt = q_ref[pl.ds(base, TILE), :]
        q = jnp.concatenate([qt[:, h * HEAD : (h + 1) * HEAD] for h in range(PART)], axis=0)
        lanes = [slice(i * 128, (i + 1) * 128) for i in range(width // 128)]
        key_iota = lax.broadcasted_iota(jnp.int32, (1, width), 1)
        s = nt_dot(q, k_ref[0, :width, :]) + jnp.where(key_iota < length, 0.0, NEG)
        most = s[:, lanes[0]]
        for cut in lanes[1:]:
            most = jnp.maximum(most, s[:, cut])
        m = jnp.broadcast_to(jnp.max(most, axis=1, keepdims=True), (many, 128)) * factor
        l = jnp.zeros((many, 128), jnp.float32)
        weights = []
        for cut in lanes:
            p = jnp.exp2(s[:, cut] * factor - m)
            l = l + p
            weights.append(p.astype(jnp.bfloat16))
        acc = jnp.dot(
            jnp.concatenate(weights, axis=1),
            v_ref[0, :width, :],
            preferred_element_type=jnp.float32,
        )
        l = jnp.sum(l, axis=1, keepdims=True)
        at_row = row_iota + base
        mine = (at_row >= start) & (at_row < start + count)
        rows = pl.ds(base, TILE)
        tops = stat_ref[0, 0, rows, :]
        sums = stat_ref[0, 1, rows, :]
        for h in range(PART):
            part = slice(h * TILE, (h + 1) * TILE)
            columns = slice(h * HEAD, (h + 1) * HEAD)
            acc_ref[0, rows, columns] = jnp.where(mine, acc[part], acc_ref[0, rows, columns])
            here = mine & (lane == h)
            tops = jnp.where(here, m[part], tops)
            sums = jnp.where(here, l[part], sums)
        stat_ref[0, 0, rows, :] = tops
        stat_ref[0, 1, rows, :] = sums
        return carry

    for n in range(1, k_ref.shape[1] // CHUNK + 1):

        @pl.when(units == n)
        def _():
            lax.fori_loop(0, tiles, functools.partial(tile, n * CHUNK), 0)


def cached_attention(info, queries, cache_key, cache_value, part, before, first=0, many=REQ):
    rows = queries.shape[0]
    wide = PART * HEAD
    parts = queries.shape[1] // wide
    head = part * PART // GROUP
    slots = cache_key.shape[1]
    extra = [] if before is None else list(before)
    carry_on = first > 0
    acc_spec = pl.BlockSpec((1, rows, wide), lambda r, s: (part, 0, 0))
    stat_spec = pl.BlockSpec((1, 2, rows, 128), lambda r, s: (part, 0, 0, 0))
    cache = pl.BlockSpec((1, slots, HEAD), lambda r, s: (r + first, 0, head))
    aliased = [acc_spec, stat_spec] if carry_on else [pl.BlockSpec(memory_space=pltpu.HBM)] * 2
    return pl.pallas_call(
        functools.partial(cached_kernel, first, carry_on),
        grid_spec=pltpu.PrefetchScalarGridSpec(
            num_scalar_prefetch=1,
            grid=(many,),
            in_specs=[pl.BlockSpec((rows, wide), lambda r, s: (0, part)), cache, cache]
            + (aliased if extra else []),
            out_specs=[acc_spec, stat_spec],
        ),
        out_shape=[
            jax.ShapeDtypeStruct((parts, rows, wide), jnp.float32),
            jax.ShapeDtypeStruct((parts, 2, rows, 128), jnp.float32),
        ],
        input_output_aliases={4: 0, 5: 1} if extra else {},
        compiler_params=params("arbitrary"),
        cost_estimate=pl.CostEstimate(
            flops=4 * rows * wide * 4096,
            bytes_accessed=6 * 1024 * 1024,
            transcendentals=rows * PART * 2048,
        ),
        name="cached_attention",
    )(info, queries, cache_key, cache_value, *extra)


def low_rank_kernel(pick, n_pieces, place, infos, *refs):
    tokens = refs[:4]
    pieces = refs[4 : 4 + n_pieces]
    before = refs[4 + n_pieces : -3]
    outs = refs[-3 - (8 if pick == "early" else 4) : -3]
    token_scr, piece_scr, sems = refs[-3:]
    rows, width = token_scr.shape[1:]
    held = piece_scr.shape[1]
    column = pl.multiple_of(place[2] * width, 128)
    copies = []
    at = 0
    for p in range(n_pieces):
        if len(pieces[p].shape) == 4:
            target = piece_scr.at[pl.ds(at, pieces[p].shape[0])]
            at += pieces[p].shape[0]
        else:
            target = piece_scr.at[at]
            at += 1
        copies.append(pltpu.make_async_copy(pieces[p], target, sems.at[8 + p]))
    sources = [tokens[0].at[:, pl.ds(column, width)]]
    sources += [tokens[n].at[pl.ds(0, rows)] for n in range(1, 4)]
    of_chip = [
        [pltpu.make_async_copy(sources[n], token_scr.at[n], sems.at[n])] for n in range(4)
    ]
    if pick == "late":
        for n in range(4):
            of_chip[n].append(pltpu.make_async_copy(before[n], outs[n], sems.at[4 + n]))
    for copy in copies + [c for n in range(4) for c in of_chip[n]]:
        copy.start()
    if pick == "early":
        for n in range(4):
            outs[n][...] = jnp.zeros_like(outs[n])
    for copy in copies:
        copy.wait()
    window = rows // 3 + ALIGN
    row_iota = lax.broadcasted_iota(jnp.int32, (window, 1), 0)
    z, y = place[0], place[1]
    at_end = (z == 0) | (z == 3)

    for n in range(4):

        def product(start, count, index, place_in):
            base = pl.multiple_of(jnp.minimum((start // ALIGN) * ALIGN, rows - window), ALIGN)
            span = pl.ds(base, window)
            low = jnp.dot(
                token_scr[n, span, :],
                piece_scr[index, place_in, :width, :],
                preferred_element_type=jnp.float32,
            )
            mine = (row_iota + base >= start) & (row_iota + base < start + count)
            outs[n][span, :] = jnp.where(mine, low, outs[n][span, :])

        for copy in of_chip[n]:
            copy.wait()
        found = [[jnp.int32(0)] * 3 for _ in range(2)]
        start = jnp.int32(0)
        for r in range(REQ):
            count = infos[n, r]
            slot = infos[n, REQ + r]
            owner = slot // held
            place_in = slot % held
            layer = owner // 2
            other = jnp.where(owner % 2 != y, 1, 0)
            mates = layer // 2 == z // 2
            ends = (layer == 0) | (layer == 3)
            last = at_end & ends & jnp.logical_not(mates)
            if pick == "early":
                kind = jnp.where(at_end, 4, jnp.where(ends, 3, 2))
                kind = jnp.where(mates, jnp.where(layer == z, 0, 1), kind)
                index = kind * 2 + other
                product(start, jnp.where(last, 0, count), index, place_in)
                outs[4 + n][r] = jnp.where(
                    last, before[0][other, place_in], piece_scr[index, place_in, width:, :]
                )
            else:
                for o in range(2):
                    here = last & (other == o)
                    fresh = (start, count, place_in)
                    found[o] = [jnp.where(here, f, g) for f, g in zip(fresh, found[o])]
            start = start + count
        if pick == "late":
            for o in range(2):
                product(found[o][0], found[o][1], o, found[o][2])


def low_rank_step(pick, place, infos, tokens, pieces, before, width):
    rows = tokens[0].shape[0]
    held, tall, rank = pieces[0].shape[-3:]
    vmem = pl.BlockSpec(memory_space=pltpu.VMEM)
    smem = pl.BlockSpec(memory_space=pltpu.SMEM)
    hbm = pl.BlockSpec(memory_space=pltpu.HBM)
    total = sum(p.shape[0] if p.ndim == 4 else 1 for p in pieces)
    ups = []
    if pick == "early":
        ups = [jax.ShapeDtypeStruct((REQ, tall - width, rank), jnp.bfloat16)] * 4
    return pl.pallas_call(
        functools.partial(low_rank_kernel, pick, len(pieces)),
        in_specs=[smem, smem]
        + [hbm] * (4 + len(pieces))
        + [vmem if pick == "early" else hbm] * len(before),
        out_specs=[vmem] * (4 + len(ups)),
        out_shape=[jax.ShapeDtypeStruct((rows, rank), jnp.float32)] * 4 + ups,
        scratch_shapes=[
            pltpu.VMEM((4, rows, width), jnp.bfloat16),
            pltpu.VMEM((total, held, tall, rank), jnp.bfloat16),
            pltpu.SemaphoreType.DMA((8 + len(pieces),)),
        ],
        compiler_params=params(),
        cost_estimate=pl.CostEstimate(
            flops=2 * 4 * rows * width * rank * 4, bytes_accessed=6 * 1024 * 1024, transcendentals=0
        ),
        name="low_rank_" + pick,
    )(place, infos, *tokens, *pieces, *before)


def final_kernel(
    info, mine_ref, other_ref, pk_ref, pv_ref, up0, up1, up2, up3, cos_ref, sin_ref, q_ref, acc_ref,
    stat_ref, ctx_ref, ko_ref, vo_ref, up_scr,
):
    rows = q_ref.shape[0]

    @pl.when(pl.program_id(0) % (GROUP // PART) == 0)
    def _():
        low = (mine_ref[...] + other_ref[...]).astype(jnp.bfloat16)
        at_row = lax.broadcasted_iota(jnp.int32, (rows, 1), 0)
        key_lin = pk_ref[...]
        value_lin = pv_ref[...]
        for n, ref in enumerate((up0, up1, up2, up3)):
            up_scr[n] = ref[...]
        tall = RANK // 2
        which = pl.ds(
            pl.multiple_of(pl.program_id(0) // (GROUP // PART) * tall, tall), tall
        )
        for r in range(REQ):
            mine = (at_row >= info[0, r]) & (at_row < info[0, r] + info[1, r])
            up = [up_scr[info[2, c], r, which, :] for c in range(4)]
            up_key = jnp.concatenate(up[:2], axis=0)
            up_value = jnp.concatenate(up[2:], axis=0)
            dk = jnp.dot(low[:, :RANK], up_key, preferred_element_type=jnp.float32)
            dv = jnp.dot(low[:, RANK:], up_value, preferred_element_type=jnp.float32)
            key_lin = key_lin + SCALE * jnp.where(mine, dk, 0.0)
            value_lin = value_lin + SCALE * jnp.where(mine, dv, 0.0)
        turned = key_lin * cos_ref[...] + pltpu.roll(key_lin, HEAD // 2, 1) * sin_ref[...]
        ko_ref[...] = turned.astype(jnp.bfloat16)
        vo_ref[...] = value_lin.astype(jnp.bfloat16)

    factor = HEAD**-0.5 * LOG2E
    most = rows // 3
    span = 2 * most

    def block(b, carry):
        low_key = pl.multiple_of(jnp.maximum(b - 1, 0) * most, most)
        at = pl.multiple_of(b * most, most)
        q_at = lax.broadcasted_iota(jnp.int32, (most, 1), 0) + at
        k_at = lax.broadcasted_iota(jnp.int32, (1, span), 1) + low_key
        q_req = jnp.zeros((most, 1), jnp.int32)
        k_req = jnp.zeros((1, span), jnp.int32)
        for r in range(1, REQ):
            q_req = q_req + (q_at >= info[0, r]).astype(jnp.int32)
            k_req = k_req + (k_at >= info[0, r]).astype(jnp.int32)
        bias = jnp.where((q_req == k_req) & (k_at <= q_at), 0.0, NEG)
        part = pl.ds(at, most)
        lane = lax.broadcasted_iota(jnp.int32, (most, 128), 1)
        heads = [slice(h * HEAD, (h + 1) * HEAD) for h in range(PART)]
        cuts = [slice(h * most, (h + 1) * most) for h in range(PART)]
        q = jnp.concatenate([q_ref[part, h] for h in heads], axis=0)
        scores = nt_dot(q, ko_ref[pl.ds(low_key, span), :])
        fresh_top = jnp.zeros((most, 128), jnp.float32)
        fresh_sum = jnp.ones((most, 128), jnp.float32)
        weights = []
        for h in range(PART):
            s = scores[cuts[h]] * factor + bias
            top = jnp.max(s, axis=1, keepdims=True)
            p = jnp.exp2(s - top)
            fresh_top = jnp.where(lane == h, top, fresh_top)
            fresh_sum = jnp.where(lane == h, jnp.sum(p, axis=1, keepdims=True), fresh_sum)
            weights.append(p.astype(jnp.bfloat16))
        fresh = jnp.dot(
            jnp.concatenate(weights, axis=0),
            vo_ref[pl.ds(low_key, span), :],
            preferred_element_type=jnp.float32,
        )
        live = lane < PART
        before = jnp.where(live, stat_ref[0, 0, part, :], 0.0)
        before_sum = jnp.where(live, stat_ref[0, 1, part, :], 1.0)
        top = jnp.maximum(before, fresh_top)
        old = jnp.exp2(before - top)
        new = jnp.exp2(fresh_top - top)
        total = before_sum * old + fresh_sum * new
        old = old / total
        new = new / total
        for h in range(PART):
            out = (
                acc_ref[0, part, heads[h]] * old[:, h : h + 1]
                + fresh[cuts[h]] * new[:, h : h + 1]
            )
            ctx_ref[part, heads[h]] = out.astype(jnp.bfloat16)
        return carry

    lax.fori_loop(0, 3, block, 0)


def final_step(info, mine, other, pk, pv, ups, cosine, sine, queries, acc, stat):
    rows = queries.shape[0]
    wide = PART * HEAD
    parts = queries.shape[1] // wide
    each = GROUP // PART
    heads = parts // each
    rank2 = mine.shape[1]
    whole = lambda shape: pl.BlockSpec(shape, lambda i, s: (0,) * len(shape))
    of_head = pl.BlockSpec((rows, HEAD), lambda i, s: (0, i // each))
    return pl.pallas_call(
        final_kernel,
        grid_spec=pltpu.PrefetchScalarGridSpec(
            num_scalar_prefetch=1,
            grid=(parts,),
            in_specs=[
                whole((rows, rank2)),
                whole((rows, rank2)),
                of_head,
                of_head,
                *([whole(ups[0].shape)] * 4),
                whole((rows, HEAD)),
                whole((rows, HEAD)),
                pl.BlockSpec((rows, wide), lambda i, s: (0, i)),
                pl.BlockSpec((1, rows, wide), lambda i, s: (i, 0, 0)),
                pl.BlockSpec((1, 2, rows, 128), lambda i, s: (i, 0, 0, 0)),
            ],
            out_specs=[pl.BlockSpec((rows, wide), lambda i, s: (0, i)), of_head, of_head],
            scratch_shapes=[pltpu.VMEM((4, *ups[0].shape), jnp.bfloat16)],
        ),
        out_shape=[
            jax.ShapeDtypeStruct(queries.shape, jnp.bfloat16),
            jax.ShapeDtypeStruct((rows, heads * HEAD), jnp.bfloat16),
            jax.ShapeDtypeStruct((rows, heads * HEAD), jnp.bfloat16),
        ],
        compiler_params=params("arbitrary", vmem=VMEM // 2),
        name="final_step",
    )(info, mine, other, pk, pv, *ups, cosine, sine, queries, acc, stat)


def after(value, *others):
    return lax.optimization_barrier((value, *others))[0]


def body(
    fast,
    tokens,
    queries,
    stored_key_cache,
    stored_value_cache,
    key_weight_matrix,
    value_weight_matrix,
    adapter_down_weight,
    adapter_up_weight,
    adapter_slot_index,
    request_adapter_index,
    fresh_token_count,
    cache_token_length,
):
    group = lax.axis_index("groups")
    replica = lax.axis_index("replica")
    core = lax.axis_index("tensor")
    rows, width = tokens.shape
    held, half, rank2 = adapter_down_weight.shape
    counts = fresh_token_count[0]
    lengths = cache_token_length[0]
    order = jnp.arange(REQ, dtype=jnp.int32)
    starts = jnp.sum(jnp.where(order[:, None] > order[None, :], counts[None, :], 0), axis=1)
    wanted = lax.dynamic_index_in_dim(request_adapter_index, replica, 0, False)
    n_slots = adapter_slot_index.shape[0]
    slots = jnp.sum(
        jnp.where(
            wanted[:, None] == jnp.arange(n_slots, dtype=jnp.int32)[None, :],
            adapter_slot_index[None, :],
            0,
        ),
        axis=1,
    )
    here = group * 2 + replica % 2 if fast else 0
    info = jnp.stack([starts, counts, order ^ here, lengths]).astype(jnp.int32)

    at_row = jnp.arange(rows, dtype=jnp.int32)
    of_request = jnp.sum(at_row[:, None] >= starts[None, 1:], axis=1)
    shift = lengths - starts
    position = at_row + jnp.sum(
        jnp.where(of_request[:, None] == jnp.arange(REQ)[None, :], shift[None, :], 0), axis=1
    )
    frequency = THETA ** (-(jnp.arange(HEAD // 2, dtype=jnp.float32) * 2.0) / HEAD)
    angles = position.astype(jnp.float32)[:, None] * frequency
    cosine = jnp.cos(angles)
    sine = jnp.sin(angles)
    cosine = jnp.concatenate([cosine, cosine], axis=1)
    sine = jnp.concatenate([-sine, sine], axis=1)

    n_replica = lax.axis_size("replica")
    tall = RANK // 2

    if fast:
        y = replica % 2
        column = group * 2 + y
        quarter = half // 4
        by_x = lambda a: lax.ppermute(a, "groups", [(0, 1), (1, 0)])
        by_y = lambda a: lax.ppermute(a, "replica", [(r, r ^ 1) for r in range(n_replica)])
        by_xy = lambda a: lax.ppermute(
            a,
            ("groups", "replica"),
            [
                (g * n_replica + r, (1 - g) * n_replica + (r ^ 1))
                for g in range(2)
                for r in range(n_replica)
            ],
        )
        mesh_z = lambda a, pairs: lax.ppermute(
            a, "replica", [(2 * f + p, 2 * t + p) for f, t in pairs for p in range(2)]
        )
        in_pair = lambda a: mesh_z(a, [(0, 1), (1, 0), (2, 3), (3, 2)])
        across = lambda a: mesh_z(a, [(1, 2), (2, 1)])
        outward = lambda a: mesh_z(a, [(1, 0), (2, 3)])

        def factor_part(c, factors):
            down = lax.dynamic_slice_in_dim(factors, c * quarter, quarter, 1)
            up = lax.dynamic_slice(
                adapter_up_weight,
                (0, c // 2, (c % 2) * tall, 0),
                (held, 1, tall, adapter_up_weight.shape[3]),
            )[:, 0]
            return jnp.concatenate([down, up[:, :, :HEAD], up[:, :, HEAD:]], axis=1)

        to_mate = factor_part(column ^ 1, adapter_down_weight)
        own_b = by_y(to_mate)
        own_a = factor_part(column, after(adapter_down_weight, to_mate))
        pair_a = in_pair(own_a)
        mid_a = across(own_a)
        note = jnp.concatenate([counts, slots])
        below = jnp.pad(note.astype(jnp.bfloat16)[None, :], ((0, 15), (0, quarter - 2 * REQ)))
        token_part = lambda c: jnp.concatenate(
            [lax.dynamic_slice_in_dim(tokens, core * half + c * quarter, quarter, 1), below]
        )
        for_x, for_y, for_d = (token_part(column ^ c) for c in (2, 1, 3))
        t_x = by_x(for_x)
        own_b, for_y, for_d = lax.optimization_barrier((own_b, for_y, for_d))
        t_y = by_y(for_y)
        t_d = by_xy(for_d)
        tokens_later = after(tokens, own_b)
        far_up = mesh_z(jnp.stack([own_a[:, quarter:], own_b[:, quarter:]]), [(0, 3), (3, 0)])
        pair_b = in_pair(own_b)
        mid_b = across(own_b)
        plain_key = jnp.dot(tokens_later, key_weight_matrix, preferred_element_type=jnp.float32)
        part = lambda n, q, b, *span: cached_attention(
            info, q, stored_key_cache, stored_value_cache, n, b, *span
        )
        across_2 = across(after(jnp.stack([pair_a, pair_b]), plain_key))
        outward_2 = outward(after(jnp.stack([mid_a, mid_b]), plain_key))
        cached = part(0, after(queries, pair_b, mid_b, far_up, t_x, plain_key), None)
        outward_3 = outward(after(across_2, cached[0]))
        plain_value = jnp.dot(
            after(tokens, cached[0]), value_weight_matrix, preferred_element_type=jnp.float32
        )
        place = jnp.stack([replica // 2, y, core * 4 + column]).astype(jnp.int32)
        t_y, t_x, t_d, _ = lax.optimization_barrier((t_y, t_x, t_d, plain_value))
        infos = jnp.stack(
            [note] + [t[rows, : 2 * REQ].astype(jnp.int32) for t in (t_y, t_x, t_d)]
        )
        layer_tokens = [tokens, t_y, t_x, t_d]
        early = [own_a, own_b, pair_a, pair_b, mid_a, mid_b, across_2, outward_2]
        low = low_rank_step("early", place, infos, layer_tokens, early, [far_up], quarter)
        ups = [low[4], by_y(low[5]), by_x(low[6]), by_xy(low[7])]
        cached = part(1, after(queries, low[0]), cached, 0, REQ // 2)
        outward_3 = after(outward_3, cached[0], *ups)
        low = low_rank_step("late", place, infos, layer_tokens, [outward_3], low[:4], quarter)
        cached = part(1, after(queries, low[0]), cached, REQ // 2, REQ // 2)
        got = [by_y(low[1]), by_x(low[2]), by_xy(low[3])]
        got = [after(g, cached[0]) for g in got]
        low_sum = low[0] + got[0] + got[1] + got[2]
    else:
        down_all = lax.all_gather(adapter_down_weight, "replica", axis=0, tiled=True)
        mine = lax.dynamic_slice_in_dim(tokens, core * half, half, 1)
        low_sum = jnp.zeros((rows, rank2), jnp.float32)
        for r in range(REQ):
            low_sum = low_sum + jnp.where(
                (of_request == r)[:, None],
                jnp.dot(mine, down_all[slots[r]], preferred_element_type=jnp.float32),
                0.0,
            )
        up_all = lax.all_gather(adapter_up_weight, "replica", axis=0, tiled=True)[slots]
        ups = []
        for c in range(4):
            up = up_all[:, c // 2, (c % 2) * tall : (c % 2 + 1) * tall]
            ups.append(jnp.concatenate([up[:, :, :HEAD], up[:, :, HEAD:]], axis=1))
        plain_key = jnp.dot(tokens, key_weight_matrix, preferred_element_type=jnp.float32)
        plain_value = jnp.dot(tokens, value_weight_matrix, preferred_element_type=jnp.float32)
        cached = None
        for n in range(queries.shape[1] // (PART * HEAD)):
            cached = cached_attention(
                info, queries, stored_key_cache, stored_value_cache, n, cached
            )
    low_other = lax.ppermute(low_sum, "tensor", [(0, 1), (1, 0)])
    return tuple(
        final_step(
            info, low_sum, low_other, plain_key, plain_value, ups, cosine, sine, queries, *cached
        )
    )


def layered(mesh):
    return dict(mesh.shape) == {"groups": 2, "replica": 8, "tensor": 2}


def solution(mesh):
    rows = P(("groups", "replica"), None)
    split = P(("groups", "replica"), "tensor")
    cache = P(("groups", "replica"), None, "tensor")
    placed = (
        rows,
        split,
        cache,
        cache,
        P(None, "tensor"),
        P(None, "tensor"),
        P("replica", "tensor", None),
        P("replica", None, None, "tensor"),
        P("groups"),
        P("groups", None),
        rows,
        rows,
    )
    return jax.shard_map(
        functools.partial(body, layered(mesh)),
        mesh=mesh,
        in_specs=placed,
        out_specs=(split, split, split),
        check_vma=False,
    )
```

```python
import functools

import jax
import jax.numpy as jnp
import numpy as np
from jax import lax
from jax.experimental import pallas as pl
from jax.experimental.pallas import tpu as pltpu
from jax.sharding import PartitionSpec as P

HEAD = 128
GROUP = 8
RANK = 64
REQ = 4
SCALE = 0.5
THETA = 500000.0
LOG2E = 1.4426950408889634
NEG = -1e30
TILE = 32
CHUNK = 512
PART = 8
ALIGN = 16
VMEM = 60 * 1024 * 1024


def params(*sem, vmem=VMEM):
    return pltpu.CompilerParams(
        dimension_semantics=sem if sem else None, vmem_limit_bytes=vmem
    )


def nt_dot(a, b):
    return lax.dot_general(a, b, (((1,), (1,)), ((), ())), preferred_element_type=jnp.float32)


def cached_kernel(first, carry_on, info, q_ref, k_ref, v_ref, *rest):
    acc_ref, stat_ref = rest[-2:]
    r = pl.program_id(0) + first
    if carry_on:

        @pl.when(pl.program_id(0) == 0)
        def _():
            acc_ref[...] = rest[0][...]
            stat_ref[...] = rest[1][...]

    rows_all = q_ref.shape[0]
    start = info[0, r]
    count = info[1, r]
    length = info[3, r]
    base0 = (start // ALIGN) * ALIGN
    tiles = (start + count - base0 + TILE - 1) // TILE
    units = (length + CHUNK - 1) // CHUNK
    factor = HEAD**-0.5 * LOG2E
    row_iota = lax.broadcasted_iota(jnp.int32, (TILE, 128), 0)
    lane = lax.broadcasted_iota(jnp.int32, (TILE, 128), 1)
    many = TILE * PART

    def tile(width, t, carry):
        base = pl.multiple_of(jnp.minimum(base0 + t * TILE, rows_all - TILE), ALIGN)
        qt = q_ref[pl.ds(base, TILE), :]
        q = jnp.concatenate([qt[:, h * HEAD : (h + 1) * HEAD] for h in range(PART)], axis=0)
        lanes = [slice(i * 128, (i + 1) * 128) for i in range(width // 128)]
        key_iota = lax.broadcasted_iota(jnp.int32, (1, width), 1)
        s = nt_dot(q, k_ref[0, :width, :]) + jnp.where(key_iota < length, 0.0, NEG)
        most = s[:, lanes[0]]
        for cut in lanes[1:]:
            most = jnp.maximum(most, s[:, cut])
        m = jnp.broadcast_to(jnp.max(most, axis=1, keepdims=True), (many, 128)) * factor
        l = jnp.zeros((many, 128), jnp.float32)
        weights = []
        for cut in lanes:
            p = jnp.exp2(s[:, cut] * factor - m)
            l = l + p
            weights.append(p.astype(jnp.bfloat16))
        acc = jnp.dot(
            jnp.concatenate(weights, axis=1),
            v_ref[0, :width, :],
            preferred_element_type=jnp.float32,
        )
        l = jnp.sum(l, axis=1, keepdims=True)
        at_row = row_iota + base
        mine = (at_row >= start) & (at_row < start + count)
        rows = pl.ds(base, TILE)
        tops = stat_ref[0, 0, rows, :]
        sums = stat_ref[0, 1, rows, :]
        for h in range(PART):
            part = slice(h * TILE, (h + 1) * TILE)
            columns = slice(h * HEAD, (h + 1) * HEAD)
            acc_ref[0, rows, columns] = jnp.where(mine, acc[part], acc_ref[0, rows, columns])
            here = mine & (lane == h)
            tops = jnp.where(here, m[part], tops)
            sums = jnp.where(here, l[part], sums)
        stat_ref[0, 0, rows, :] = tops
        stat_ref[0, 1, rows, :] = sums
        return carry

    for n in range(1, k_ref.shape[1] // CHUNK + 1):

        @pl.when(units == n)
        def _():
            lax.fori_loop(0, tiles, functools.partial(tile, n * CHUNK), 0)


def cached_attention(info, queries, cache_key, cache_value, part, before, first=0, many=REQ):
    rows = queries.shape[0]
    wide = PART * HEAD
    parts = queries.shape[1] // wide
    head = part * PART // GROUP
    slots = cache_key.shape[1]
    extra = [] if before is None else list(before)
    carry_on = first > 0
    acc_spec = pl.BlockSpec((1, rows, wide), lambda r, s: (part, 0, 0))
    stat_spec = pl.BlockSpec((1, 2, rows, 128), lambda r, s: (part, 0, 0, 0))
    cache = pl.BlockSpec((1, slots, HEAD), lambda r, s: (r + first, 0, head))
    aliased = [acc_spec, stat_spec] if carry_on else [pl.BlockSpec(memory_space=pltpu.HBM)] * 2
    return pl.pallas_call(
        functools.partial(cached_kernel, first, carry_on),
        grid_spec=pltpu.PrefetchScalarGridSpec(
            num_scalar_prefetch=1,
            grid=(many,),
            in_specs=[pl.BlockSpec((rows, wide), lambda r, s: (0, part)), cache, cache]
            + (aliased if extra else []),
            out_specs=[acc_spec, stat_spec],
        ),
        out_shape=[
            jax.ShapeDtypeStruct((parts, rows, wide), jnp.float32),
            jax.ShapeDtypeStruct((parts, 2, rows, 128), jnp.float32),
        ],
        input_output_aliases={4: 0, 5: 1} if extra else {},
        compiler_params=params("arbitrary"),
        cost_estimate=pl.CostEstimate(
            flops=4 * rows * wide * 4096,
            bytes_accessed=6 * 1024 * 1024,
            transcendentals=rows * PART * 2048,
        ),
        name="cached_attention",
    )(info, queries, cache_key, cache_value, *extra)


def low_rank_kernel(pick, n_pieces, place, infos, *refs):
    tokens = refs[:4]
    pieces = refs[4 : 4 + n_pieces]
    before = refs[4 + n_pieces : -3]
    outs = refs[-3 - (8 if pick == "early" else 4) : -3]
    token_scr, piece_scr, sems = refs[-3:]
    rows, width = token_scr.shape[1:]
    held = piece_scr.shape[1]
    column = pl.multiple_of(place[2] * width, 128)
    copies = []
    at = 0
    for p in range(n_pieces):
        if len(pieces[p].shape) == 4:
            target = piece_scr.at[pl.ds(at, pieces[p].shape[0])]
            at += pieces[p].shape[0]
        else:
            target = piece_scr.at[at]
            at += 1
        copies.append(pltpu.make_async_copy(pieces[p], target, sems.at[8 + p]))
    sources = [tokens[0].at[:, pl.ds(column, width)]]
    sources += [tokens[n].at[pl.ds(0, rows)] for n in range(1, 4)]
    of_chip = [
        [pltpu.make_async_copy(sources[n], token_scr.at[n], sems.at[n])] for n in range(4)
    ]
    if pick == "late":
        for n in range(4):
            of_chip[n].append(pltpu.make_async_copy(before[n], outs[n], sems.at[4 + n]))
    for copy in copies + [c for n in range(4) for c in of_chip[n]]:
        copy.start()
    if pick == "early":
        for n in range(4):
            outs[n][...] = jnp.zeros_like(outs[n])
    for copy in copies:
        copy.wait()
    window = rows // 3 + ALIGN
    row_iota = lax.broadcasted_iota(jnp.int32, (window, 1), 0)
    z, y = place[0], place[1]
    at_end = (z == 0) | (z == 3)

    for n in range(4):

        def product(start, count, index, place_in):
            base = pl.multiple_of(jnp.minimum((start // ALIGN) * ALIGN, rows - window), ALIGN)
            span = pl.ds(base, window)
            low = jnp.dot(
                token_scr[n, span, :],
                piece_scr[index, place_in, :width, :],
                preferred_element_type=jnp.float32,
            )
            mine = (row_iota + base >= start) & (row_iota + base < start + count)
            outs[n][span, :] = jnp.where(mine, low, outs[n][span, :])

        for copy in of_chip[n]:
            copy.wait()
        found = [[jnp.int32(0)] * 3 for _ in range(2)]
        start = jnp.int32(0)
        for r in range(REQ):
            count = infos[n, r]
            slot = infos[n, REQ + r]
            owner = slot // held
            place_in = slot % held
            layer = owner // 2
            other = jnp.where(owner % 2 != y, 1, 0)
            mates = layer // 2 == z // 2
            ends = (layer == 0) | (layer == 3)
            last = at_end & ends & jnp.logical_not(mates)
            if pick == "early":
                kind = jnp.where(at_end, 4, jnp.where(ends, 3, 2))
                kind = jnp.where(mates, jnp.where(layer == z, 0, 1), kind)
                index = kind * 2 + other
                product(start, jnp.where(last, 0, count), index, place_in)
                outs[4 + n][r] = jnp.where(
                    last, before[0][other, place_in], piece_scr[index, place_in, width:, :]
                )
            else:
                for o in range(2):
                    here = last & (other == o)
                    fresh = (start, count, place_in)
                    found[o] = [jnp.where(here, f, g) for f, g in zip(fresh, found[o])]
            start = start + count
        if pick == "late":
            for o in range(2):
                product(found[o][0], found[o][1], o, found[o][2])


def low_rank_step(pick, place, infos, tokens, pieces, before, width):
    rows = tokens[0].shape[0]
    held, tall, rank = pieces[0].shape[-3:]
    vmem = pl.BlockSpec(memory_space=pltpu.VMEM)
    smem = pl.BlockSpec(memory_space=pltpu.SMEM)
    hbm = pl.BlockSpec(memory_space=pltpu.HBM)
    total = sum(p.shape[0] if p.ndim == 4 else 1 for p in pieces)
    ups = []
    if pick == "early":
        ups = [jax.ShapeDtypeStruct((REQ, tall - width, rank), jnp.bfloat16)] * 4
    return pl.pallas_call(
        functools.partial(low_rank_kernel, pick, len(pieces)),
        in_specs=[smem, smem]
        + [hbm] * (4 + len(pieces))
        + [vmem if pick == "early" else hbm] * len(before),
        out_specs=[vmem] * (4 + len(ups)),
        out_shape=[jax.ShapeDtypeStruct((rows, rank), jnp.float32)] * 4 + ups,
        scratch_shapes=[
            pltpu.VMEM((4, rows, width), jnp.bfloat16),
            pltpu.VMEM((total, held, tall, rank), jnp.bfloat16),
            pltpu.SemaphoreType.DMA((8 + len(pieces),)),
        ],
        compiler_params=params(),
        cost_estimate=pl.CostEstimate(
            flops=2 * 4 * rows * width * rank * 4, bytes_accessed=6 * 1024 * 1024, transcendentals=0
        ),
        name="low_rank_" + pick,
    )(place, infos, *tokens, *pieces, *before)


def final_kernel(
    info, mine_ref, other_ref, pk_ref, pv_ref, up0, up1, up2, up3, cos_ref, sin_ref, q_ref, acc_ref,
    stat_ref, ctx_ref, ko_ref, vo_ref, up_scr,
):
    rows = q_ref.shape[0]

    @pl.when(pl.program_id(0) % (GROUP // PART) == 0)
    def _():
        low = (mine_ref[...] + other_ref[...]).astype(jnp.bfloat16)
        at_row = lax.broadcasted_iota(jnp.int32, (rows, 1), 0)
        key_lin = pk_ref[...]
        value_lin = pv_ref[...]
        for n, ref in enumerate((up0, up1, up2, up3)):
            up_scr[n] = ref[...]
        tall = RANK // 2
        which = pl.ds(
            pl.multiple_of(pl.program_id(0) // (GROUP // PART) * tall, tall), tall
        )
        for r in range(REQ):
            mine = (at_row >= info[0, r]) & (at_row < info[0, r] + info[1, r])
            up = [up_scr[info[2, c], r, which, :] for c in range(4)]
            up_key = jnp.concatenate(up[:2], axis=0)
            up_value = jnp.concatenate(up[2:], axis=0)
            dk = jnp.dot(low[:, :RANK], up_key, preferred_element_type=jnp.float32)
            dv = jnp.dot(low[:, RANK:], up_value, preferred_element_type=jnp.float32)
            key_lin = key_lin + SCALE * jnp.where(mine, dk, 0.0)
            value_lin = value_lin + SCALE * jnp.where(mine, dv, 0.0)
        turned = key_lin * cos_ref[...] + pltpu.roll(key_lin, HEAD // 2, 1) * sin_ref[...]
        ko_ref[...] = turned.astype(jnp.bfloat16)
        vo_ref[...] = value_lin.astype(jnp.bfloat16)

    factor = HEAD**-0.5 * LOG2E
    most = rows // 3
    span = 2 * most

    def block(b, carry):
        low_key = pl.multiple_of(jnp.maximum(b - 1, 0) * most, most)
        at = pl.multiple_of(b * most, most)
        q_at = lax.broadcasted_iota(jnp.int32, (most, 1), 0) + at
        k_at = lax.broadcasted_iota(jnp.int32, (1, span), 1) + low_key
        q_req = jnp.zeros((most, 1), jnp.int32)
        k_req = jnp.zeros((1, span), jnp.int32)
        for r in range(1, REQ):
            q_req = q_req + (q_at >= info[0, r]).astype(jnp.int32)
            k_req = k_req + (k_at >= info[0, r]).astype(jnp.int32)
        bias = jnp.where((q_req == k_req) & (k_at <= q_at), 0.0, NEG)
        part = pl.ds(at, most)
        lane = lax.broadcasted_iota(jnp.int32, (most, 128), 1)
        heads = [slice(h * HEAD, (h + 1) * HEAD) for h in range(PART)]
        cuts = [slice(h * most, (h + 1) * most) for h in range(PART)]
        q = jnp.concatenate([q_ref[part, h] for h in heads], axis=0)
        scores = nt_dot(q, ko_ref[pl.ds(low_key, span), :])
        fresh_top = jnp.zeros((most, 128), jnp.float32)
        fresh_sum = jnp.ones((most, 128), jnp.float32)
        weights = []
        for h in range(PART):
            s = scores[cuts[h]] * factor + bias
            top = jnp.max(s, axis=1, keepdims=True)
            p = jnp.exp2(s - top)
            fresh_top = jnp.where(lane == h, top, fresh_top)
            fresh_sum = jnp.where(lane == h, jnp.sum(p, axis=1, keepdims=True), fresh_sum)
            weights.append(p.astype(jnp.bfloat16))
        fresh = jnp.dot(
            jnp.concatenate(weights, axis=0),
            vo_ref[pl.ds(low_key, span), :],
            preferred_element_type=jnp.float32,
        )
        live = lane < PART
        before = jnp.where(live, stat_ref[0, 0, part, :], 0.0)
        before_sum = jnp.where(live, stat_ref[0, 1, part, :], 1.0)
        top = jnp.maximum(before, fresh_top)
        old = jnp.exp2(before - top)
        new = jnp.exp2(fresh_top - top)
        total = before_sum * old + fresh_sum * new
        old = old / total
        new = new / total
        for h in range(PART):
            out = (
                acc_ref[0, part, heads[h]] * old[:, h : h + 1]
                + fresh[cuts[h]] * new[:, h : h + 1]
            )
            ctx_ref[part, heads[h]] = out.astype(jnp.bfloat16)
        return carry

    lax.fori_loop(0, 3, block, 0)


def final_step(info, mine, other, pk, pv, ups, cosine, sine, queries, acc, stat):
    rows = queries.shape[0]
    wide = PART * HEAD
    parts = queries.shape[1] // wide
    each = GROUP // PART
    heads = parts // each
    rank2 = mine.shape[1]
    whole = lambda shape: pl.BlockSpec(shape, lambda i, s: (0,) * len(shape))
    of_head = pl.BlockSpec((rows, HEAD), lambda i, s: (0, i // each))
    return pl.pallas_call(
        final_kernel,
        grid_spec=pltpu.PrefetchScalarGridSpec(
            num_scalar_prefetch=1,
            grid=(parts,),
            in_specs=[
                whole((rows, rank2)),
                whole((rows, rank2)),
                of_head,
                of_head,
                *([whole(ups[0].shape)] * 4),
                whole((rows, HEAD)),
                whole((rows, HEAD)),
                pl.BlockSpec((rows, wide), lambda i, s: (0, i)),
                pl.BlockSpec((1, rows, wide), lambda i, s: (i, 0, 0)),
                pl.BlockSpec((1, 2, rows, 128), lambda i, s: (i, 0, 0, 0)),
            ],
            out_specs=[pl.BlockSpec((rows, wide), lambda i, s: (0, i)), of_head, of_head],
            scratch_shapes=[pltpu.VMEM((4, *ups[0].shape), jnp.bfloat16)],
        ),
        out_shape=[
            jax.ShapeDtypeStruct(queries.shape, jnp.bfloat16),
            jax.ShapeDtypeStruct((rows, heads * HEAD), jnp.bfloat16),
            jax.ShapeDtypeStruct((rows, heads * HEAD), jnp.bfloat16),
        ],
        compiler_params=params("arbitrary", vmem=VMEM // 2),
        name="final_step",
    )(info, mine, other, pk, pv, *ups, cosine, sine, queries, acc, stat)


def after(value, *others):
    return lax.optimization_barrier((value, *others))[0]


def body(
    fast,
    tokens,
    queries,
    stored_key_cache,
    stored_value_cache,
    key_weight_matrix,
    value_weight_matrix,
    adapter_down_weight,
    adapter_up_weight,
    adapter_slot_index,
    request_adapter_index,
    fresh_token_count,
    cache_token_length,
):
    group = lax.axis_index("groups")
    replica = lax.axis_index("replica")
    core = lax.axis_index("tensor")
    rows, width = tokens.shape
    held, half, rank2 = adapter_down_weight.shape
    counts = fresh_token_count[0]
    lengths = cache_token_length[0]
    order = jnp.arange(REQ, dtype=jnp.int32)
    starts = jnp.sum(jnp.where(order[:, None] > order[None, :], counts[None, :], 0), axis=1)
    wanted = lax.dynamic_index_in_dim(request_adapter_index, replica, 0, False)
    n_slots = adapter_slot_index.shape[0]
    slots = jnp.sum(
        jnp.where(
            wanted[:, None] == jnp.arange(n_slots, dtype=jnp.int32)[None, :],
            adapter_slot_index[None, :],
            0,
        ),
        axis=1,
    )
    here = group * 2 + replica % 2 if fast else 0
    info = jnp.stack([starts, counts, order ^ here, lengths]).astype(jnp.int32)

    at_row = jnp.arange(rows, dtype=jnp.int32)
    of_request = jnp.sum(at_row[:, None] >= starts[None, 1:], axis=1)
    shift = lengths - starts
    position = at_row + jnp.sum(
        jnp.where(of_request[:, None] == jnp.arange(REQ)[None, :], shift[None, :], 0), axis=1
    )
    frequency = THETA ** (-(jnp.arange(HEAD // 2, dtype=jnp.float32) * 2.0) / HEAD)
    angles = position.astype(jnp.float32)[:, None] * frequency
    cosine = jnp.cos(angles)
    sine = jnp.sin(angles)
    cosine = jnp.concatenate([cosine, cosine], axis=1)
    sine = jnp.concatenate([-sine, sine], axis=1)

    n_replica = lax.axis_size("replica")
    tall = RANK // 2

    if fast:
        y = replica % 2
        column = group * 2 + y
        quarter = half // 4
        by_x = lambda a: lax.ppermute(a, "groups", [(0, 1), (1, 0)])
        by_y = lambda a: lax.ppermute(a, "replica", [(r, r ^ 1) for r in range(n_replica)])
        by_xy = lambda a: lax.ppermute(
            a,
            ("groups", "replica"),
            [
                (g * n_replica + r, (1 - g) * n_replica + (r ^ 1))
                for g in range(2)
                for r in range(n_replica)
            ],
        )
        mesh_z = lambda a, pairs: lax.ppermute(
            a, "replica", [(2 * f + p, 2 * t + p) for f, t in pairs for p in range(2)]
        )
        in_pair = lambda a: mesh_z(a, [(0, 1), (1, 0), (2, 3), (3, 2)])
        across = lambda a: mesh_z(a, [(1, 2), (2, 1)])
        outward = lambda a: mesh_z(a, [(1, 0), (2, 3)])

        def factor_part(c, factors):
            down = lax.dynamic_slice_in_dim(factors, c * quarter, quarter, 1)
            up = lax.dynamic_slice(
                adapter_up_weight,
                (0, c // 2, (c % 2) * tall, 0),
                (held, 1, tall, adapter_up_weight.shape[3]),
            )[:, 0]
            return jnp.concatenate([down, up[:, :, :HEAD], up[:, :, HEAD:]], axis=1)

        to_mate = factor_part(column ^ 1, adapter_down_weight)
        own_b = by_y(to_mate)
        own_a = factor_part(column, after(adapter_down_weight, to_mate))
        pair_a = in_pair(own_a)
        mid_a = across(own_a)
        note = jnp.concatenate([counts, slots])
        below = jnp.pad(note.astype(jnp.bfloat16)[None, :], ((0, 15), (0, quarter - 2 * REQ)))
        token_part = lambda c: jnp.concatenate(
            [lax.dynamic_slice_in_dim(tokens, core * half + c * quarter, quarter, 1), below]
        )
        for_x, for_y, for_d = (token_part(column ^ c) for c in (2, 1, 3))
        t_x = by_x(for_x)
        own_b, for_y, for_d = lax.optimization_barrier((own_b, for_y, for_d))
        t_y = by_y(for_y)
        t_d = by_xy(for_d)
        tokens_later = after(tokens, own_b)
        far_up = mesh_z(jnp.stack([own_a[:, quarter:], own_b[:, quarter:]]), [(0, 3), (3, 0)])
        pair_b = in_pair(own_b)
        mid_b = across(own_b)
        plain_key = jnp.dot(tokens_later, key_weight_matrix, preferred_element_type=jnp.float32)
        part = lambda n, q, b, *span: cached_attention(
            info, q, stored_key_cache, stored_value_cache, n, b, *span
        )
        to_cross = after(jnp.stack([pair_a, pair_b]), plain_key)
        across_2 = across(to_cross)
        outward_2 = outward(after(jnp.stack([after(mid_a, to_cross), mid_b]), plain_key))
        cached = part(0, after(queries, pair_b, mid_b, far_up, t_x, plain_key), None)
        outward_3 = outward(after(across_2, cached[0]))
        plain_value = jnp.dot(
            after(tokens, cached[0]), value_weight_matrix, preferred_element_type=jnp.float32
        )
        place = jnp.stack([replica // 2, y, core * 4 + column]).astype(jnp.int32)
        t_y, t_x, t_d, _ = lax.optimization_barrier((t_y, t_x, t_d, plain_value))
        infos = jnp.stack(
            [note] + [t[rows, : 2 * REQ].astype(jnp.int32) for t in (t_y, t_x, t_d)]
        )
        layer_tokens = [tokens, t_y, t_x, t_d]
        early = [own_a, own_b, pair_a, pair_b, mid_a, mid_b, across_2, outward_2]
        low = low_rank_step("early", place, infos, layer_tokens, early, [far_up], quarter)
        ups = [low[4], by_y(low[5]), by_x(low[6]), by_xy(low[7])]
        cached = part(1, after(queries, low[0]), cached, 0, REQ // 2)
        outward_3 = after(outward_3, cached[0], *ups)
        low = low_rank_step("late", place, infos, layer_tokens, [outward_3], low[:4], quarter)
        cached = part(1, after(queries, low[0]), cached, REQ // 2, REQ // 2)
        got = [by_y(low[1]), by_x(low[2]), by_xy(low[3])]
        got = [after(g, cached[0]) for g in got]
        low_sum = low[0] + got[0] + got[1] + got[2]
    else:
        down_all = lax.all_gather(adapter_down_weight, "replica", axis=0, tiled=True)
        mine = lax.dynamic_slice_in_dim(tokens, core * half, half, 1)
        low_sum = jnp.zeros((rows, rank2), jnp.float32)
        for r in range(REQ):
            low_sum = low_sum + jnp.where(
                (of_request == r)[:, None],
                jnp.dot(mine, down_all[slots[r]], preferred_element_type=jnp.float32),
                0.0,
            )
        up_all = lax.all_gather(adapter_up_weight, "replica", axis=0, tiled=True)[slots]
        ups = []
        for c in range(4):
            up = up_all[:, c // 2, (c % 2) * tall : (c % 2 + 1) * tall]
            ups.append(jnp.concatenate([up[:, :, :HEAD], up[:, :, HEAD:]], axis=1))
        plain_key = jnp.dot(tokens, key_weight_matrix, preferred_element_type=jnp.float32)
        plain_value = jnp.dot(tokens, value_weight_matrix, preferred_element_type=jnp.float32)
        cached = None
        for n in range(queries.shape[1] // (PART * HEAD)):
            cached = cached_attention(
                info, queries, stored_key_cache, stored_value_cache, n, cached
            )
    low_other = lax.ppermute(low_sum, "tensor", [(0, 1), (1, 0)])
    return tuple(
        final_step(
            info, low_sum, low_other, plain_key, plain_value, ups, cosine, sine, queries, *cached
        )
    )


def layered(mesh):
    return dict(mesh.shape) == {"groups": 2, "replica": 8, "tensor": 2}


def solution(mesh):
    rows = P(("groups", "replica"), None)
    split = P(("groups", "replica"), "tensor")
    cache = P(("groups", "replica"), None, "tensor")
    placed = (
        rows,
        split,
        cache,
        cache,
        P(None, "tensor"),
        P(None, "tensor"),
        P("replica", "tensor", None),
        P("replica", None, None, "tensor"),
        P("groups"),
        P("groups", None),
        rows,
        rows,
    )
    return jax.shard_map(
        functools.partial(body, layered(mesh)),
        mesh=mesh,
        in_specs=placed,
        out_specs=(split, split, split),
        check_vma=False,
    )
```

```python
import functools

import jax
import jax.numpy as jnp
import numpy as np
from jax import lax
from jax.experimental import pallas as pl
from jax.experimental.pallas import tpu as pltpu
from jax.sharding import PartitionSpec as P

HEAD = 128
GROUP = 8
RANK = 64
REQ = 4
SCALE = 0.5
THETA = 500000.0
LOG2E = 1.4426950408889634
NEG = -1e30
TILE = 32
CHUNK = 256
PART = 8
ALIGN = 16
VMEM = 60 * 1024 * 1024


def params(*sem, vmem=VMEM):
    return pltpu.CompilerParams(
        dimension_semantics=sem if sem else None, vmem_limit_bytes=vmem
    )


def nt_dot(a, b):
    return lax.dot_general(a, b, (((1,), (1,)), ((), ())), preferred_element_type=jnp.float32)


def cached_kernel(first, carry_on, info, q_ref, k_ref, v_ref, *rest):
    acc_ref, stat_ref = rest[-2:]
    r = pl.program_id(0) + first
    if carry_on:

        @pl.when(pl.program_id(0) == 0)
        def _():
            acc_ref[...] = rest[0][...]
            stat_ref[...] = rest[1][...]

    rows_all = q_ref.shape[0]
    start = info[0, r]
    count = info[1, r]
    length = info[3, r]
    base0 = (start // ALIGN) * ALIGN
    tiles = (start + count - base0 + TILE - 1) // TILE
    units = (length + CHUNK - 1) // CHUNK
    factor = HEAD**-0.5 * LOG2E
    row_iota = lax.broadcasted_iota(jnp.int32, (TILE, 128), 0)
    lane = lax.broadcasted_iota(jnp.int32, (TILE, 128), 1)
    many = TILE * PART

    def tile(width, t, carry):
        base = pl.multiple_of(jnp.minimum(base0 + t * TILE, rows_all - TILE), ALIGN)
        qt = q_ref[pl.ds(base, TILE), :]
        q = jnp.concatenate([qt[:, h * HEAD : (h + 1) * HEAD] for h in range(PART)], axis=0)
        lanes = [slice(i * 128, (i + 1) * 128) for i in range(width // 128)]
        key_iota = lax.broadcasted_iota(jnp.int32, (1, width), 1)
        s = nt_dot(q, k_ref[0, :width, :]) + jnp.where(key_iota < length, 0.0, NEG)
        most = s[:, lanes[0]]
        for cut in lanes[1:]:
            most = jnp.maximum(most, s[:, cut])
        m = jnp.broadcast_to(jnp.max(most, axis=1, keepdims=True), (many, 128)) * factor
        l = jnp.zeros((many, 128), jnp.float32)
        weights = []
        for cut in lanes:
            p = jnp.exp2(s[:, cut] * factor - m)
            l = l + p
            weights.append(p.astype(jnp.bfloat16))
        acc = jnp.dot(
            jnp.concatenate(weights, axis=1),
            v_ref[0, :width, :],
            preferred_element_type=jnp.float32,
        )
        l = jnp.sum(l, axis=1, keepdims=True)
        at_row = row_iota + base
        mine = (at_row >= start) & (at_row < start + count)
        rows = pl.ds(base, TILE)
        tops = stat_ref[0, 0, rows, :]
        sums = stat_ref[0, 1, rows, :]
        for h in range(PART):
            part = slice(h * TILE, (h + 1) * TILE)
            columns = slice(h * HEAD, (h + 1) * HEAD)
            acc_ref[0, rows, columns] = jnp.where(mine, acc[part], acc_ref[0, rows, columns])
            here = mine & (lane == h)
            tops = jnp.where(here, m[part], tops)
            sums = jnp.where(here, l[part], sums)
        stat_ref[0, 0, rows, :] = tops
        stat_ref[0, 1, rows, :] = sums
        return carry

    for n in range(1, k_ref.shape[1] // CHUNK + 1):

        @pl.when(units == n)
        def _():
            lax.fori_loop(0, tiles, functools.partial(tile, n * CHUNK), 0)


def cached_attention(info, queries, cache_key, cache_value, part, before, first=0, many=REQ):
    rows = queries.shape[0]
    wide = PART * HEAD
    parts = queries.shape[1] // wide
    head = part * PART // GROUP
    slots = cache_key.shape[1]
    extra = [] if before is None else list(before)
    carry_on = first > 0
    acc_spec = pl.BlockSpec((1, rows, wide), lambda r, s: (part, 0, 0))
    stat_spec = pl.BlockSpec((1, 2, rows, 128), lambda r, s: (part, 0, 0, 0))
    cache = pl.BlockSpec((1, slots, HEAD), lambda r, s: (r + first, 0, head))
    aliased = [acc_spec, stat_spec] if carry_on else [pl.BlockSpec(memory_space=pltpu.HBM)] * 2
    return pl.pallas_call(
        functools.partial(cached_kernel, first, carry_on),
        grid_spec=pltpu.PrefetchScalarGridSpec(
            num_scalar_prefetch=1,
            grid=(many,),
            in_specs=[pl.BlockSpec((rows, wide), lambda r, s: (0, part)), cache, cache]
            + (aliased if extra else []),
            out_specs=[acc_spec, stat_spec],
        ),
        out_shape=[
            jax.ShapeDtypeStruct((parts, rows, wide), jnp.float32),
            jax.ShapeDtypeStruct((parts, 2, rows, 128), jnp.float32),
        ],
        input_output_aliases={4: 0, 5: 1} if extra else {},
        compiler_params=params("arbitrary"),
        cost_estimate=pl.CostEstimate(
            flops=4 * rows * wide * 4096,
            bytes_accessed=6 * 1024 * 1024,
            transcendentals=rows * PART * 2048,
        ),
        name="cached_attention",
    )(info, queries, cache_key, cache_value, *extra)


def low_rank_kernel(pick, n_pieces, place, infos, *refs):
    tokens = refs[:4]
    pieces = refs[4 : 4 + n_pieces]
    before = refs[4 + n_pieces : -3]
    outs = refs[-3 - (8 if pick == "early" else 4) : -3]
    token_scr, piece_scr, sems = refs[-3:]
    rows, width = token_scr.shape[1:]
    held = piece_scr.shape[1]
    column = pl.multiple_of(place[2] * width, 128)
    copies = []
    at = 0
    for p in range(n_pieces):
        if len(pieces[p].shape) == 4:
            target = piece_scr.at[pl.ds(at, pieces[p].shape[0])]
            at += pieces[p].shape[0]
        else:
            target = piece_scr.at[at]
            at += 1
        copies.append(pltpu.make_async_copy(pieces[p], target, sems.at[8 + p]))
    sources = [tokens[0].at[:, pl.ds(column, width)]]
    sources += [tokens[n].at[pl.ds(0, rows)] for n in range(1, 4)]
    of_chip = [
        [pltpu.make_async_copy(sources[n], token_scr.at[n], sems.at[n])] for n in range(4)
    ]
    if pick == "late":
        for n in range(4):
            of_chip[n].append(pltpu.make_async_copy(before[n], outs[n], sems.at[4 + n]))
    for copy in copies + [c for n in range(4) for c in of_chip[n]]:
        copy.start()
    if pick == "early":
        for n in range(4):
            outs[n][...] = jnp.zeros_like(outs[n])
    for copy in copies:
        copy.wait()
    window = rows // 3 + ALIGN
    row_iota = lax.broadcasted_iota(jnp.int32, (window, 1), 0)
    z, y = place[0], place[1]
    at_end = (z == 0) | (z == 3)

    for n in range(4):

        def product(start, count, index, place_in):
            base = pl.multiple_of(jnp.minimum((start // ALIGN) * ALIGN, rows - window), ALIGN)
            span = pl.ds(base, window)
            low = jnp.dot(
                token_scr[n, span, :],
                piece_scr[index, place_in, :width, :],
                preferred_element_type=jnp.float32,
            )
            mine = (row_iota + base >= start) & (row_iota + base < start + count)
            outs[n][span, :] = jnp.where(mine, low, outs[n][span, :])

        for copy in of_chip[n]:
            copy.wait()
        found = [[jnp.int32(0)] * 3 for _ in range(2)]
        start = jnp.int32(0)
        for r in range(REQ):
            count = infos[n, r]
            slot = infos[n, REQ + r]
            owner = slot // held
            place_in = slot % held
            layer = owner // 2
            other = jnp.where(owner % 2 != y, 1, 0)
            mates = layer // 2 == z // 2
            ends = (layer == 0) | (layer == 3)
            last = at_end & ends & jnp.logical_not(mates)
            if pick == "early":
                kind = jnp.where(at_end, 4, jnp.where(ends, 3, 2))
                kind = jnp.where(mates, jnp.where(layer == z, 0, 1), kind)
                index = kind * 2 + other
                product(start, jnp.where(last, 0, count), index, place_in)
                outs[4 + n][r] = jnp.where(
                    last, before[0][other, place_in], piece_scr[index, place_in, width:, :]
                )
            else:
                for o in range(2):
                    here = last & (other == o)
                    fresh = (start, count, place_in)
                    found[o] = [jnp.where(here, f, g) for f, g in zip(fresh, found[o])]
            start = start + count
        if pick == "late":
            for o in range(2):
                product(found[o][0], found[o][1], o, found[o][2])


def low_rank_step(pick, place, infos, tokens, pieces, before, width):
    rows = tokens[0].shape[0]
    held, tall, rank = pieces[0].shape[-3:]
    vmem = pl.BlockSpec(memory_space=pltpu.VMEM)
    smem = pl.BlockSpec(memory_space=pltpu.SMEM)
    hbm = pl.BlockSpec(memory_space=pltpu.HBM)
    total = sum(p.shape[0] if p.ndim == 4 else 1 for p in pieces)
    ups = []
    if pick == "early":
        ups = [jax.ShapeDtypeStruct((REQ, tall - width, rank), jnp.bfloat16)] * 4
    return pl.pallas_call(
        functools.partial(low_rank_kernel, pick, len(pieces)),
        in_specs=[smem, smem]
        + [hbm] * (4 + len(pieces))
        + [vmem if pick == "early" else hbm] * len(before),
        out_specs=[vmem] * (4 + len(ups)),
        out_shape=[jax.ShapeDtypeStruct((rows, rank), jnp.float32)] * 4 + ups,
        scratch_shapes=[
            pltpu.VMEM((4, rows, width), jnp.bfloat16),
            pltpu.VMEM((total, held, tall, rank), jnp.bfloat16),
            pltpu.SemaphoreType.DMA((8 + len(pieces),)),
        ],
        compiler_params=params(),
        cost_estimate=pl.CostEstimate(
            flops=2 * 4 * rows * width * rank * 4, bytes_accessed=6 * 1024 * 1024, transcendentals=0
        ),
        name="low_rank_" + pick,
    )(place, infos, *tokens, *pieces, *before)


def final_kernel(
    info, mine_ref, other_ref, pk_ref, pv_ref, up0, up1, up2, up3, cos_ref, sin_ref, q_ref, acc_ref,
    stat_ref, ctx_ref, ko_ref, vo_ref, up_scr,
):
    rows = q_ref.shape[0]

    @pl.when(pl.program_id(0) % (GROUP // PART) == 0)
    def _():
        low = (mine_ref[...] + other_ref[...]).astype(jnp.bfloat16)
        at_row = lax.broadcasted_iota(jnp.int32, (rows, 1), 0)
        key_lin = pk_ref[...]
        value_lin = pv_ref[...]
        for n, ref in enumerate((up0, up1, up2, up3)):
            up_scr[n] = ref[...]
        tall = RANK // 2
        which = pl.ds(
            pl.multiple_of(pl.program_id(0) // (GROUP // PART) * tall, tall), tall
        )
        for r in range(REQ):
            mine = (at_row >= info[0, r]) & (at_row < info[0, r] + info[1, r])
            up = [up_scr[info[2, c], r, which, :] for c in range(4)]
            up_key = jnp.concatenate(up[:2], axis=0)
            up_value = jnp.concatenate(up[2:], axis=0)
            dk = jnp.dot(low[:, :RANK], up_key, preferred_element_type=jnp.float32)
            dv = jnp.dot(low[:, RANK:], up_value, preferred_element_type=jnp.float32)
            key_lin = key_lin + SCALE * jnp.where(mine, dk, 0.0)
            value_lin = value_lin + SCALE * jnp.where(mine, dv, 0.0)
        turned = key_lin * cos_ref[...] + pltpu.roll(key_lin, HEAD // 2, 1) * sin_ref[...]
        ko_ref[...] = turned.astype(jnp.bfloat16)
        vo_ref[...] = value_lin.astype(jnp.bfloat16)

    factor = HEAD**-0.5 * LOG2E
    most = rows // 3
    span = 2 * most

    def block(b, carry):
        low_key = pl.multiple_of(jnp.maximum(b - 1, 0) * most, most)
        at = pl.multiple_of(b * most, most)
        q_at = lax.broadcasted_iota(jnp.int32, (most, 1), 0) + at
        k_at = lax.broadcasted_iota(jnp.int32, (1, span), 1) + low_key
        q_req = jnp.zeros((most, 1), jnp.int32)
        k_req = jnp.zeros((1, span), jnp.int32)
        for r in range(1, REQ):
            q_req = q_req + (q_at >= info[0, r]).astype(jnp.int32)
            k_req = k_req + (k_at >= info[0, r]).astype(jnp.int32)
        bias = jnp.where((q_req == k_req) & (k_at <= q_at), 0.0, NEG)
        part = pl.ds(at, most)
        lane = lax.broadcasted_iota(jnp.int32, (most, 128), 1)
        heads = [slice(h * HEAD, (h + 1) * HEAD) for h in range(PART)]
        cuts = [slice(h * most, (h + 1) * most) for h in range(PART)]
        q = jnp.concatenate([q_ref[part, h] for h in heads], axis=0)
        scores = nt_dot(q, ko_ref[pl.ds(low_key, span), :])
        fresh_top = jnp.zeros((most, 128), jnp.float32)
        fresh_sum = jnp.ones((most, 128), jnp.float32)
        weights = []
        for h in range(PART):
            s = scores[cuts[h]] * factor + bias
            top = jnp.max(s, axis=1, keepdims=True)
            p = jnp.exp2(s - top)
            fresh_top = jnp.where(lane == h, top, fresh_top)
            fresh_sum = jnp.where(lane == h, jnp.sum(p, axis=1, keepdims=True), fresh_sum)
            weights.append(p.astype(jnp.bfloat16))
        fresh = jnp.dot(
            jnp.concatenate(weights, axis=0),
            vo_ref[pl.ds(low_key, span), :],
            preferred_element_type=jnp.float32,
        )
        live = lane < PART
        before = jnp.where(live, stat_ref[0, 0, part, :], 0.0)
        before_sum = jnp.where(live, stat_ref[0, 1, part, :], 1.0)
        top = jnp.maximum(before, fresh_top)
        old = jnp.exp2(before - top)
        new = jnp.exp2(fresh_top - top)
        total = before_sum * old + fresh_sum * new
        old = old / total
        new = new / total
        for h in range(PART):
            out = (
                acc_ref[0, part, heads[h]] * old[:, h : h + 1]
                + fresh[cuts[h]] * new[:, h : h + 1]
            )
            ctx_ref[part, heads[h]] = out.astype(jnp.bfloat16)
        return carry

    lax.fori_loop(0, 3, block, 0)


def final_step(info, mine, other, pk, pv, ups, cosine, sine, queries, acc, stat):
    rows = queries.shape[0]
    wide = PART * HEAD
    parts = queries.shape[1] // wide
    each = GROUP // PART
    heads = parts // each
    rank2 = mine.shape[1]
    whole = lambda shape: pl.BlockSpec(shape, lambda i, s: (0,) * len(shape))
    of_head = pl.BlockSpec((rows, HEAD), lambda i, s: (0, i // each))
    return pl.pallas_call(
        final_kernel,
        grid_spec=pltpu.PrefetchScalarGridSpec(
            num_scalar_prefetch=1,
            grid=(parts,),
            in_specs=[
                whole((rows, rank2)),
                whole((rows, rank2)),
                of_head,
                of_head,
                *([whole(ups[0].shape)] * 4),
                whole((rows, HEAD)),
                whole((rows, HEAD)),
                pl.BlockSpec((rows, wide), lambda i, s: (0, i)),
                pl.BlockSpec((1, rows, wide), lambda i, s: (i, 0, 0)),
                pl.BlockSpec((1, 2, rows, 128), lambda i, s: (i, 0, 0, 0)),
            ],
            out_specs=[pl.BlockSpec((rows, wide), lambda i, s: (0, i)), of_head, of_head],
            scratch_shapes=[pltpu.VMEM((4, *ups[0].shape), jnp.bfloat16)],
        ),
        out_shape=[
            jax.ShapeDtypeStruct(queries.shape, jnp.bfloat16),
            jax.ShapeDtypeStruct((rows, heads * HEAD), jnp.bfloat16),
            jax.ShapeDtypeStruct((rows, heads * HEAD), jnp.bfloat16),
        ],
        compiler_params=params("arbitrary", vmem=VMEM // 2),
        name="final_step",
    )(info, mine, other, pk, pv, *ups, cosine, sine, queries, acc, stat)


def after(value, *others):
    return lax.optimization_barrier((value, *others))[0]


def body(
    fast,
    tokens,
    queries,
    stored_key_cache,
    stored_value_cache,
    key_weight_matrix,
    value_weight_matrix,
    adapter_down_weight,
    adapter_up_weight,
    adapter_slot_index,
    request_adapter_index,
    fresh_token_count,
    cache_token_length,
):
    group = lax.axis_index("groups")
    replica = lax.axis_index("replica")
    core = lax.axis_index("tensor")
    rows, width = tokens.shape
    held, half, rank2 = adapter_down_weight.shape
    counts = fresh_token_count[0]
    lengths = cache_token_length[0]
    order = jnp.arange(REQ, dtype=jnp.int32)
    starts = jnp.sum(jnp.where(order[:, None] > order[None, :], counts[None, :], 0), axis=1)
    wanted = lax.dynamic_index_in_dim(request_adapter_index, replica, 0, False)
    n_slots = adapter_slot_index.shape[0]
    slots = jnp.sum(
        jnp.where(
            wanted[:, None] == jnp.arange(n_slots, dtype=jnp.int32)[None, :],
            adapter_slot_index[None, :],
            0,
        ),
        axis=1,
    )
    here = group * 2 + replica % 2 if fast else 0
    info = jnp.stack([starts, counts, order ^ here, lengths]).astype(jnp.int32)

    at_row = jnp.arange(rows, dtype=jnp.int32)
    of_request = jnp.sum(at_row[:, None] >= starts[None, 1:], axis=1)
    shift = lengths - starts
    position = at_row + jnp.sum(
        jnp.where(of_request[:, None] == jnp.arange(REQ)[None, :], shift[None, :], 0), axis=1
    )
    frequency = THETA ** (-(jnp.arange(HEAD // 2, dtype=jnp.float32) * 2.0) / HEAD)
    angles = position.astype(jnp.float32)[:, None] * frequency
    cosine = jnp.cos(angles)
    sine = jnp.sin(angles)
    cosine = jnp.concatenate([cosine, cosine], axis=1)
    sine = jnp.concatenate([-sine, sine], axis=1)

    n_replica = lax.axis_size("replica")
    tall = RANK // 2

    if fast:
        y = replica % 2
        column = group * 2 + y
        quarter = half // 4
        by_x = lambda a: lax.ppermute(a, "groups", [(0, 1), (1, 0)])
        by_y = lambda a: lax.ppermute(a, "replica", [(r, r ^ 1) for r in range(n_replica)])
        by_xy = lambda a: lax.ppermute(
            a,
            ("groups", "replica"),
            [
                (g * n_replica + r, (1 - g) * n_replica + (r ^ 1))
                for g in range(2)
                for r in range(n_replica)
            ],
        )
        mesh_z = lambda a, pairs: lax.ppermute(
            a, "replica", [(2 * f + p, 2 * t + p) for f, t in pairs for p in range(2)]
        )
        in_pair = lambda a: mesh_z(a, [(0, 1), (1, 0), (2, 3), (3, 2)])
        across = lambda a: mesh_z(a, [(1, 2), (2, 1)])
        outward = lambda a: mesh_z(a, [(1, 0), (2, 3)])

        def factor_part(c, factors):
            down = lax.dynamic_slice_in_dim(factors, c * quarter, quarter, 1)
            up = lax.dynamic_slice(
                adapter_up_weight,
                (0, c // 2, (c % 2) * tall, 0),
                (held, 1, tall, adapter_up_weight.shape[3]),
            )[:, 0]
            return jnp.concatenate([down, up[:, :, :HEAD], up[:, :, HEAD:]], axis=1)

        to_mate = factor_part(column ^ 1, adapter_down_weight)
        own_b = by_y(to_mate)
        own_a = factor_part(column, after(adapter_down_weight, to_mate))
        pair_a = in_pair(own_a)
        mid_a = across(own_a)
        note = jnp.concatenate([counts, slots])
        below = jnp.pad(note.astype(jnp.bfloat16)[None, :], ((0, 15), (0, quarter - 2 * REQ)))
        token_part = lambda c: jnp.concatenate(
            [lax.dynamic_slice_in_dim(tokens, core * half + c * quarter, quarter, 1), below]
        )
        for_x, for_y, for_d = (token_part(column ^ c) for c in (2, 1, 3))
        t_x = by_x(for_x)
        own_b, for_y, for_d = lax.optimization_barrier((own_b, for_y, for_d))
        t_y = by_y(for_y)
        t_d = by_xy(for_d)
        tokens_later = after(tokens, own_b)
        far_up = mesh_z(jnp.stack([own_a[:, quarter:], own_b[:, quarter:]]), [(0, 3), (3, 0)])
        pair_b = in_pair(own_b)
        mid_b = across(own_b)
        plain_key = jnp.dot(tokens_later, key_weight_matrix, preferred_element_type=jnp.float32)
        part = lambda n, q, b, *span: cached_attention(
            info, q, stored_key_cache, stored_value_cache, n, b, *span
        )
        to_cross = after(jnp.stack([pair_a, pair_b]), plain_key)
        across_2 = across(to_cross)
        outward_2 = outward(after(jnp.stack([after(mid_a, to_cross), mid_b]), plain_key))
        cached = part(0, after(queries, pair_b, mid_b, far_up, t_x, plain_key), None)
        outward_3 = outward(after(across_2, cached[0]))
        plain_value = jnp.dot(
            after(tokens, cached[0]), value_weight_matrix, preferred_element_type=jnp.float32
        )
        place = jnp.stack([replica // 2, y, core * 4 + column]).astype(jnp.int32)
        t_y, t_x, t_d, _ = lax.optimization_barrier((t_y, t_x, t_d, plain_value))
        infos = jnp.stack(
            [note] + [t[rows, : 2 * REQ].astype(jnp.int32) for t in (t_y, t_x, t_d)]
        )
        layer_tokens = [tokens, t_y, t_x, t_d]
        early = [own_a, own_b, pair_a, pair_b, mid_a, mid_b, across_2, outward_2]
        low = low_rank_step("early", place, infos, layer_tokens, early, [far_up], quarter)
        ups = [low[4], by_y(low[5]), by_x(low[6]), by_xy(low[7])]
        cached = part(1, after(queries, low[0]), cached, 0, REQ // 2)
        outward_3 = after(outward_3, cached[0], *ups)
        low = low_rank_step("late", place, infos, layer_tokens, [outward_3], low[:4], quarter)
        cached = part(1, after(queries, low[0]), cached, REQ // 2, REQ // 2)
        got = [by_y(low[1]), by_x(low[2]), by_xy(low[3])]
        got = [after(g, cached[0]) for g in got]
        low_sum = low[0] + got[0] + got[1] + got[2]
    else:
        down_all = lax.all_gather(adapter_down_weight, "replica", axis=0, tiled=True)
        mine = lax.dynamic_slice_in_dim(tokens, core * half, half, 1)
        low_sum = jnp.zeros((rows, rank2), jnp.float32)
        for r in range(REQ):
            low_sum = low_sum + jnp.where(
                (of_request == r)[:, None],
                jnp.dot(mine, down_all[slots[r]], preferred_element_type=jnp.float32),
                0.0,
            )
        up_all = lax.all_gather(adapter_up_weight, "replica", axis=0, tiled=True)[slots]
        ups = []
        for c in range(4):
            up = up_all[:, c // 2, (c % 2) * tall : (c % 2 + 1) * tall]
            ups.append(jnp.concatenate([up[:, :, :HEAD], up[:, :, HEAD:]], axis=1))
        plain_key = jnp.dot(tokens, key_weight_matrix, preferred_element_type=jnp.float32)
        plain_value = jnp.dot(tokens, value_weight_matrix, preferred_element_type=jnp.float32)
        cached = None
        for n in range(queries.shape[1] // (PART * HEAD)):
            cached = cached_attention(
                info, queries, stored_key_cache, stored_value_cache, n, cached
            )
    low_other = lax.ppermute(low_sum, "tensor", [(0, 1), (1, 0)])
    return tuple(
        final_step(
            info, low_sum, low_other, plain_key, plain_value, ups, cosine, sine, queries, *cached
        )
    )


def layered(mesh):
    return dict(mesh.shape) == {"groups": 2, "replica": 8, "tensor": 2}


def solution(mesh):
    rows = P(("groups", "replica"), None)
    split = P(("groups", "replica"), "tensor")
    cache = P(("groups", "replica"), None, "tensor")
    placed = (
        rows,
        split,
        cache,
        cache,
        P(None, "tensor"),
        P(None, "tensor"),
        P("replica", "tensor", None),
        P("replica", None, None, "tensor"),
        P("groups"),
        P("groups", None),
        rows,
        rows,
    )
    return jax.shard_map(
        functools.partial(body, layered(mesh)),
        mesh=mesh,
        in_specs=placed,
        out_specs=(split, split, split),
        check_vma=False,
    )
```
